256 devices in a mesh: slab: 256 (over y, z, x, core).
Axes of the slice: x: 4, y: 4, z: 8, core: 2. Of those that a mesh axis runs over, the one named last changes fastest.
Arguments:
- tensor: float32 [1024, 1024, 512], P('slab'), may hold values from 0 to 1024
- first: float32 [1024, 512], P('slab'), may hold values from 0.01 to 2.01
- second: float32 [1024, 512], replicated, may hold values from 0.01 to 2.01
- third: float32 [512, 512], replicated, may hold values from 0.01 to 2.01
Outputs:
- new_first: float32 [1024, 512], P('slab')
- new_second: float32 [1024, 512], P('slab')
- new_third: float32 [512, 512], P('slab')
The draws below stay inside these ranges and needn't reach their ends.
All inputs are finite; a program needn't handle non-finite values.
Results may differ from the reference program's by a relative error of at most 0.0002.
Values sent between devices are 32-bit elements; how exact they have to be, the bound alone decides.
A program may use at most 64 MiB of HBM per device.

```python
import math
import jax
import jax.numpy as jnp
from jax import lax

J = 1024
K = 512
R = 512
I = 1024


signal_rank = 64


signal_scale = 14.0


upper_bound = 1024.0


def sparse_factor(key, row_count, col_count):
    key_mask = jax.random.fold_in(key, 101)
    key_value = jax.random.fold_in(key, 202)
    fraction = 0.125
    magnitude = 2.0 * jax.random.uniform(key_value, (row_count, col_count), jnp.float32)
    keep_mask = (jax.random.uniform(key_mask, (row_count, col_count), jnp.float32) < fraction).astype(jnp.float32)
    return 0.01 + keep_mask * magnitude


def draw_tensor(key, part):
    left_factor = sparse_factor(jax.random.fold_in(key, 11), I, signal_rank)
    middle_factor = sparse_factor(jax.random.fold_in(key, 12), J, signal_rank)
    right_factor = sparse_factor(jax.random.fold_in(key, 13), K, signal_rank)
    paired = (left_factor[:, None, :] * middle_factor[None, :, :]).reshape(I * J, signal_rank)
    signal = jnp.dot(paired, right_factor.T, precision=lax.Precision.HIGHEST).reshape(I, J, K)
    noise_part = jax.random.uniform(jax.random.fold_in(key, 14), (I, J, K), jnp.float32)
    return jnp.minimum(signal_scale * signal + noise_part, upper_bound)


def draw_first(key, part):
    return sparse_factor(jax.random.fold_in(key, 21), I, R)


def draw_second(key, part):
    return sparse_factor(jax.random.fold_in(key, 22), J, R)


def draw_third(key, part):
    return sparse_factor(jax.random.fold_in(key, 23), K, R)


def setup_inputs(seed: int = 0) -> dict:
    key_of = jax.random.split(jax.random.key(seed), 5)
    tensor = draw_tensor(jax.random.fold_in(key_of[4], 71), 0)
    first = draw_first(jax.random.fold_in(key_of[4], 71), 0)
    second = draw_second(jax.random.fold_in(key_of[4], 71), 0)
    third = draw_third(jax.random.fold_in(key_of[4], 71), 0)
    return {"tensor": tensor, "first": first, "second": second, "third": third}


def update(start_rows, sums, gram):
    highest = lax.Precision.HIGHEST
    lipschitz = jnp.max(jnp.sum(gram, axis=1))
    previous = start_rows
    extrapolated = start_rows
    updated = start_rows
    for turn in range(4):
        gradient = jnp.dot(extrapolated, gram, precision=highest) - sums
        updated = jnp.maximum(extrapolated - gradient / lipschitz, 0.0)
        extrapolated = updated + (turn / (turn + 3.0)) * (updated - previous)
        previous = updated
    return updated


def reference(tensor, first, second, third):
    highest = lax.Precision.HIGHEST
    rows_block = math.gcd(I, 32)
    blocks_count = I // rows_block
    slab_blocks = tensor.reshape(blocks_count, rows_block, J, K)
    gram_second = jnp.dot(second.T, second, precision=highest)
    gram_third = jnp.dot(third.T, third, precision=highest)

    def mode_one(slab_block):
        partial_value = jnp.einsum('ijk,kr->ijr', slab_block, third, precision=highest)
        return jnp.einsum('ijr,jr->ir', partial_value, second, precision=highest)

    first_sums = lax.map(mode_one, slab_blocks).reshape(I, R)
    new_first = update(first, first_sums, gram_second * gram_third)
    gram_first = jnp.dot(new_first.T, new_first, precision=highest)
    first_blocks = new_first.reshape(blocks_count, rows_block, R)

    def mode_two(totals, paired):
        slab_block, own_rows = paired
        partial_value = jnp.einsum('ijk,kr->ijr', slab_block, third, precision=highest)
        return totals + jnp.einsum('ijr,ir->jr', partial_value, own_rows, precision=highest), None

    second_sums, _ = lax.scan(mode_two, jnp.zeros((J, R), jnp.float32), (slab_blocks, first_blocks))
    new_second = update(second, second_sums, gram_first * gram_third)
    gram_new_second = jnp.dot(new_second.T, new_second, precision=highest)

    def mode_three(totals, paired):
        slab_block, own_rows = paired
        weighted = new_second[None, :, :] * own_rows[:, None, :]
        return totals + jnp.einsum('ijk,ijr->kr', slab_block, weighted, precision=highest), None

    third_sums, _ = lax.scan(mode_three, jnp.zeros((K, R), jnp.float32), (slab_blocks, first_blocks))
    new_third = update(third, third_sums, gram_first * gram_new_second)
    return (new_first, new_second, new_third)
```

```python
import functools

import jax
import jax.numpy as jnp
from jax import lax
from jax.experimental import pallas as pl
from jax.experimental.pallas import tpu as pltpu
from jax.sharding import PartitionSpec as P

F32 = jnp.float32
BF16 = jnp.bfloat16
MESH = pl.DeviceIdType.MESH
GRIDS = {256: (4, 4, 8), 16: (2, 2, 2)}


def mm(a, b):
    return lax.dot_general(a, b, (((1,), (0,)), ((), ())), preferred_element_type=F32)


def split(v):
    hi = v.astype(BF16)
    return hi, (v - hi.astype(F32)).astype(BF16)


def sum8(v):
    rows, cols = v.shape
    return jnp.sum(v.reshape(rows // 8, 8, cols), axis=0)


class Shape:
    def __init__(self, devices, K, R):
        self.NX, self.NY, self.NZ = GRIDS[devices]
        self.J = 8 * self.NX * self.NY * self.NZ
        self.K, self.R = K, R
        self.Q = R // 4

    def reduce_scratch(self, tag, blocks):
        NX, NY, NZ, Q = self.NX, self.NY, self.NZ, self.Q
        ra, rb, zb = NY * blocks * 8, NX * blocks * 8, blocks * 8
        dma = pltpu.SemaphoreType.DMA
        out = {
            "pa": pltpu.VMEM((2, NX, ra, Q), F32),
            "pb": pltpu.VMEM((2, NY, rb, Q), F32),
            "ca": pltpu.VMEM((NX, ra, Q), F32),
            "cb": pltpu.VMEM((NY, rb, Q), F32),
            "sa": pltpu.VMEM((NX, ra, Q), F32),
            "sb": pltpu.VMEM((NY, rb, Q), F32),
            "r1a": pltpu.VMEM((NX - 1, ra, Q), F32),
            "r1b": pltpu.VMEM((NY - 1, rb, Q), F32),
            "s2a": pltpu.VMEM((NY, zb, Q), F32),
            "s2b": pltpu.VMEM((NX, zb, Q), F32),
            "r2a": pltpu.VMEM((NY - 1, zb, Q), F32),
            "r2b": pltpu.VMEM((NX - 1, zb, Q), F32),
            "zs": pltpu.VMEM((blocks, 16, Q), F32),
            "rz": pltpu.VMEM((NZ - 1, 16, Q), F32),
            "mh": pltpu.VMEM((2, 16, Q), F32),
        }
        for name, count in (("c", NX + NY), ("1a", NX - 1), ("1b", NY - 1), ("2a", NY - 1), ("2b", NX - 1), ("z", NZ - 1), ("m", 1)):
            out["send_" + name] = dma((count,))
            out["recv_" + name] = dma((count,))
        return {tag + k: v for k, v in out.items()}

    def gather_scratch(self, tag):
        NX, NY, NZ, Q = self.NX, self.NY, self.NZ, self.Q
        dma = pltpu.SemaphoreType.DMA
        out = {
            "zg": pltpu.VMEM((NZ, 16, Q), F32),
            "ga": pltpu.VMEM((2, NX, NY, NZ * 8, Q), F32),
            "gb": pltpu.VMEM((2, NY, NX, NZ * 8, Q), F32),
        }
        for name, count in (("z", NZ - 1), ("2a", NY - 1), ("2b", NX - 1), ("3a", NX - 1), ("3b", NY - 1), ("c", NX + NY)):
            out["send_" + name] = dma((count,))
            out["recv_" + name] = dma((count,))
        return {tag + k: v for k, v in out.items()}

    def scratch(self):
        J, K, R, NX, NY, NZ = self.J, self.K, self.R, self.NX, self.NY, self.NZ
        dma = pltpu.SemaphoreType.DMA
        out = {
            "t": pltpu.VMEM((4, NX, NY, NZ, 8, K), F32),
            "second": pltpu.VMEM((NX, NY, NZ, 8, R), F32),
            "third": pltpu.VMEM((K, R), F32),
            "p": pltpu.VMEM((4, J, R), F32),
            "b3": pltpu.VMEM((3 * K, R), BF16),
            "tt_hi": pltpu.VMEM((4, K, J), BF16),
            "tt_lo": pltpu.VMEM((4, K, J), BF16),
            "s3": pltpu.VMEM((3 * J, R), BF16),
            "st": pltpu.VMEM((R, J), BF16),
            "gram_c": pltpu.VMEM((R, R), F32),
            "gram_a": pltpu.VMEM((R, R), F32),
            "gram_b": pltpu.VMEM((R, R), F32),
            "cross": pltpu.VMEM((R, R), F32),
            "q3": pltpu.VMEM((K, R), F32),
            "gx": pltpu.VMEM((R, 2 * R), BF16),
            "fs": pltpu.VMEM((4, 8, R), F32),
            "f8": pltpu.VMEM((2, 4, R), F32),
            "load_t": dma((4 * NX,)),
            "load_s": dma((NX,)),
            "load_b": dma((1,)),
            "send_f": dma((1,)),
            "recv_f": dma((1,)),
        }
        out.update(self.reduce_scratch("u_", NZ))
        out.update(self.reduce_scratch("v_", NZ // 2))
        out.update(self.gather_scratch("f_"))
        out.update(self.gather_scratch("g_"))
        return out


class Place:
    def __init__(self, shape):
        self.shape = shape
        me = lax.axis_index("slab")
        self.core = lax.rem(me, 2)
        self.x = lax.rem(me // 2, shape.NX)
        self.z = lax.rem(me // (2 * shape.NX), shape.NZ)
        self.y = me // (2 * shape.NX * shape.NZ)

    def device(self, dx=0, dy=0, dz=0, dc=0):
        s = self.shape
        x, y, z = lax.rem(self.x + dx, s.NX), lax.rem(self.y + dy, s.NY), lax.rem(self.z + dz, s.NZ)
        core = lax.rem(self.core + dc, 2)
        return ((y * s.NZ + z) * s.NX + x) * 2 + core

    def partners(self):
        s = self.shape
        return (
            [self.device(dx=d) for d in range(1, s.NX)]
            + [self.device(dy=d) for d in range(1, s.NY)]
            + [self.device(dz=d) for d in range(1, s.NZ)]
            + [self.device(dc=1)]
        )


def remote(src, dst, send, recv, device):
    return pltpu.make_async_remote_copy(src, dst, send, recv, device_id=(device,), device_id_type=MESH)


class Reduce:
    def __init__(self, m, tag, place, blocks):
        self.m = {k[len(tag):]: v for k, v in m.items() if k.startswith(tag)}
        self.place, self.blocks, self.sends = place, blocks, []

    def start(self, src, dst, sem, k, device):
        copy = remote(src, dst, self.m["send_" + sem].at[k], self.m["recv_" + sem].at[k], device)
        copy.start()
        self.sends.append(copy)

    def wait(self, dst, sem, k):
        remote(dst, dst, self.m["send_" + sem].at[k], self.m["recv_" + sem].at[k], self.place.device()).wait_recv()

    def core_send(self, part, a):
        m, place = self.m, self.place
        k = a if part == "a" else place.shape.NX + a
        self.start(m["p" + part].at[1 - place.core, a], m["c" + part].at[a], "c", k, place.device(dc=1))

    def stage1(self):
        m, place, s = self.m, self.place, self.place.shape
        for d in range(1, max(s.NX, s.NY) + 1):
            for part, n, at in (("a", s.NX, place.x), ("b", s.NY, place.y)):
                if d > n:
                    continue
                a = lax.rem(at + d, n)
                self.wait(m["c" + part].at[a], "c", a if part == "a" else s.NX + a)
                m["s" + part][a] = m["p" + part][place.core, a] + m["c" + part][a]
                if d < n:
                    to = place.device(dx=d) if part == "a" else place.device(dy=d)
                    self.start(m["s" + part].at[a], m["r1" + part].at[d - 1], "1" + part, d - 1, to)

    def stage2(self):
        m, place, s = self.m, self.place, self.place.shape
        zb = self.blocks * 8
        for part, n1, at1, n2, at2 in (("a", s.NX, place.x, s.NY, place.y), ("b", s.NY, place.y, s.NX, place.x)):
            for d in range(n1 - 1):
                self.wait(m["r1" + part].at[d], "1" + part, d)
            for e in range(1, n2 + 1):
                b = lax.rem(at2 + e, n2)
                rows = pl.ds(pl.multiple_of(b * zb, 8), zb)
                total = m["s" + part][at1, rows]
                for d in range(n1 - 1):
                    total = total + m["r1" + part][d, rows]
                m["s2" + part][b] = total
                if e < n2:
                    to = place.device(dy=e) if part == "a" else place.device(dx=e)
                    self.start(m["s2" + part].at[b], m["r2" + part].at[e - 1], "2" + part, e - 1, to)

    def stage3(self):
        m, place, s = self.m, self.place, self.place.shape
        for half, (part, n2, at2) in enumerate((("a", s.NY, place.y), ("b", s.NX, place.x))):
            for e in range(n2 - 1):
                self.wait(m["r2" + part].at[e], "2" + part, e)
            total = m["s2" + part][at2]
            for e in range(n2 - 1):
                total = total + m["r2" + part][e]
            m["zs"][:, half * 8 : half * 8 + 8] = total.reshape(self.blocks, 8, s.Q)
        per = s.NZ // self.blocks
        for d in range(1, s.NZ):
            block = lax.rem(place.z + d, s.NZ) // per
            self.start(m["zs"].at[block], m["rz"].at[d - 1], "z", d - 1, place.device(dz=d))

    def finish(self):
        m, place, s = self.m, self.place, self.place.shape
        per = s.NZ // self.blocks
        total = m["zs"][place.z // per]
        for d in range(s.NZ - 1):
            self.wait(m["rz"].at[d], "z", d)
            total = total + m["rz"][d]
        m["mh"][place.core] = total
        self.start(m["mh"].at[place.core], m["mh"].at[place.core], "m", 0, place.device(dc=1))
        self.wait(m["mh"].at[1 - place.core], "m", 0)
        out = jnp.concatenate([m["mh"][h, q * 8 : q * 8 + 8] for h in range(2) for q in range(2)], axis=1)
        for copy in self.sends:
            copy.wait_send()
        return out


class Gather:
    def __init__(self, m, tag, place):
        self.m = {k[len(tag):]: v for k, v in m.items() if k.startswith(tag)}
        self.place, self.sends = place, []

    start = Reduce.start
    wait = Reduce.wait

    def stage1(self, rows):
        m, place, s = self.m, self.place, self.place.shape
        Q = s.Q
        own = jnp.where(place.core == 0, rows[:, : 2 * Q], rows[:, 2 * Q :])
        m["zg"][place.z] = jnp.concatenate([own[:, :Q], own[:, Q:]], axis=0)
        for d in range(1, s.NZ):
            self.start(m["zg"].at[place.z], m["zg"].at[place.z], "z", d - 1, place.device(dz=d))

    def stage2(self):
        m, place, s = self.m, self.place, self.place.shape
        for d in range(1, s.NZ):
            self.wait(m["zg"].at[lax.rem(place.z + s.NZ - d, s.NZ)], "z", d - 1)
        m["ga"][place.core, place.x, place.y] = m["zg"][:, 0:8].reshape(s.NZ * 8, s.Q)
        m["gb"][place.core, place.y, place.x] = m["zg"][:, 8:16].reshape(s.NZ * 8, s.Q)
        for e in range(1, s.NY):
            ref = m["ga"].at[place.core, place.x, place.y]
            self.start(ref, ref, "2a", e - 1, place.device(dy=e))
        for e in range(1, s.NX):
            ref = m["gb"].at[place.core, place.y, place.x]
            self.start(ref, ref, "2b", e - 1, place.device(dx=e))

    def stage3(self):
        m, place, s = self.m, self.place, self.place.shape
        for e in range(1, s.NY):
            self.wait(m["ga"].at[place.core, place.x, lax.rem(place.y + s.NY - e, s.NY)], "2a", e - 1)
        ref = m["ga"].at[place.core, place.x]
        for d in range(1, s.NX):
            self.start(ref, ref, "3a", d - 1, place.device(dx=d))
        for e in range(1, s.NX):
            self.wait(m["gb"].at[place.core, place.y, lax.rem(place.x + s.NX - e, s.NX)], "2b", e - 1)
        other = m["gb"].at[place.core, place.y]
        for d in range(1, s.NY):
            self.start(other, other, "3b", d - 1, place.device(dy=d))
        self.start(ref, ref, "c", 0, place.device(dc=1))
        self.start(other, other, "c", s.NX, place.device(dc=1))

    def stage4(self):
        m, place, s = self.m, self.place, self.place.shape
        for d in range(1, max(s.NX, s.NY)):
            if d < s.NX:
                ref = m["ga"].at[place.core, lax.rem(place.x + s.NX - d, s.NX)]
                self.wait(ref, "3a", d - 1)
                self.start(ref, ref, "c", d, place.device(dc=1))
            if d < s.NY:
                ref = m["gb"].at[place.core, lax.rem(place.y + s.NY - d, s.NY)]
                self.wait(ref, "3b", d - 1)
                self.start(ref, ref, "c", s.NX + d, place.device(dc=1))

    def finish(self):
        m, place, s = self.m, self.place, self.place.shape
        for d in range(s.NX):
            self.wait(m["ga"].at[1 - place.core, lax.rem(place.x + s.NX - d, s.NX)], "c", d)
        for d in range(s.NY):
            self.wait(m["gb"].at[1 - place.core, lax.rem(place.y + s.NY - d, s.NY)], "c", s.NX + d)
        for copy in self.sends:
            copy.wait_send()

    def assemble(self, s3, st):
        m, s = self.m, self.place.shape
        J, Q, rows = s.J, s.Q, s.NZ * 8
        per = s.NY * rows

        def step(x, carry):
            for h in range(2):
                for part in range(2):
                    cols = slice((h * 2 + part) * Q, (h * 2 + part + 1) * Q)
                    if part == 0:
                        v = m["ga"][h, x].reshape(per, Q)
                    else:
                        v = jnp.concatenate([m["gb"][h, y, x] for y in range(s.NY)], axis=0)
                    hi, lo = split(v)
                    at = pl.multiple_of(x * per, per)
                    s3[pl.ds(at, per), cols] = hi
                    s3[pl.ds(J + at, per), cols] = lo
                    s3[pl.ds(2 * J + at, per), cols] = hi
                    st[cols, pl.ds(at, per)] = v.T.astype(BF16)
            return carry

        for x in range(s.NX):
            step(x, 0)


def gram_of(st, s3, rows, out, cross):
    hi, lo = s3[0:rows, :], s3[rows : 2 * rows, :]
    t = st[:, 0:rows]
    cross[...] = mm(t, lo)
    out[...] = mm(t, hi)
    out[...] = out[...] + cross[...] + cross[...].T


def load_factor(get, rows, block, s3, st):
    for at in range(0, rows, block):
        v = get(at)
        hi, lo = split(v)
        s3[at : at + block, :] = hi
        s3[rows + at : rows + at + block, :] = lo
        s3[2 * rows + at : 2 * rows + at + block, :] = hi
        st[:, at : at + block] = v.T.astype(BF16)


def set_gram(g, gx):
    hi, lo = split(g)
    R = g.shape[0]
    gx[:, 0:R] = hi
    gx[:, R : 2 * R] = lo
    return 1.0 / jnp.max(jnp.sum(g, axis=0, keepdims=True), axis=1, keepdims=True)


def update(rows, sums, gx, inverse):
    n, R = rows.shape
    previous = extrapolated = updated = rows
    for turn in range(4):
        hi = extrapolated.astype(BF16).astype(F32)
        both = jnp.concatenate([hi, extrapolated - hi], axis=0).astype(BF16)
        product = mm(both, gx[...])
        product = product[:n] + product[n:]
        product = product[:, :R] + product[:, R:]
        updated = jnp.maximum(extrapolated - (product - sums) * inverse, 0.0)
        if turn < 3:
            extrapolated = updated + turn / (turn + 3.0) * (updated - previous)
            previous = updated
    return updated


def kernel(shape, names, tensor, first, second, third, out_first, out_second, out_third, *refs):
    m = dict(zip(names, refs))
    s, place = shape, Place(shape)
    J, K, R, NX, NY, NZ, Q = s.J, s.K, s.R, s.NX, s.NY, s.NZ, s.Q
    per = NY * NZ * 8

    load_b = pltpu.make_async_copy(third, m["third"], m["load_b"].at[0])
    load_b.start()

    def load_t(i, x):
        return pltpu.make_async_copy(tensor.at[i, :, :, x], m["t"].at[i, x], m["load_t"].at[i * NX + x])

    def load_s(x):
        return pltpu.make_async_copy(second.at[:, :, x], m["second"].at[x], m["load_s"].at[x])

    for x in range(NX):
        load_t(0, x).start()
    for x in range(NX):
        load_s(x).start()
    for i in range(1, 4):
        for x in range(NX):
            load_t(i, x).start()

    barrier = pltpu.get_barrier_semaphore()
    partners = place.partners()
    for device in partners:
        pl.semaphore_signal(barrier, inc=1, device_id=(device,), device_id_type=MESH)

    load_b.wait()
    load_factor(lambda at: m["third"][at : at + K // 4, :], K, K // 4, m["b3"], m["st"])
    gram_of(m["st"], m["b3"], K, m["gram_c"], m["cross"])
    for x in range(NX):
        load_s(x).wait()

    m["fs"][...] = jnp.zeros_like(m["fs"])

    def product(step, carry):
        i, x = step // NX, lax.rem(step, NX)
        load_t(i, x).wait()
        hi, lo = split(m["t"][i, x].reshape(per, K))
        p = mm(jnp.concatenate([hi, hi, lo], axis=1), m["b3"][...])
        m["p"][i, pl.ds(pl.multiple_of(x * per, per), per), :] = p
        m["fs"][i] += sum8(p * m["second"][x].reshape(per, R))
        return carry

    lax.fori_loop(0, 4 * NX, product, 0)

    load_factor(lambda at: m["second"][at // per].reshape(per, R), J, per, m["s3"], m["st"])
    gram_of(m["st"], m["s3"], J, m["gram_b"], m["cross"])
    inverse = set_gram(m["gram_b"][...] * m["gram_c"][...], m["gx"])
    sums = jnp.concatenate([jnp.sum(m["fs"][i], axis=0, keepdims=True) for i in range(4)] * 2, axis=0)
    start = first[...]
    rows = update(jnp.concatenate([start, start], axis=0), sums, m["gx"], inverse)
    new_first = rows[0:4]
    out_first[...] = new_first

    pl.semaphore_wait(barrier, len(partners))
    m["f8"][place.core] = new_first
    copy_f = remote(m["f8"].at[place.core], m["f8"].at[place.core], m["send_f"].at[0], m["recv_f"].at[0], place.device(dc=1))
    copy_f.start()

    u = Reduce(m, "u_", place, NZ)
    v = Reduce(m, "v_", place, NZ // 2)
    f = Gather(m, "f_", place)
    g = Gather(m, "g_", place)

    def weighted(at, count, cols):
        total = m["p"][0, pl.ds(pl.multiple_of(at, 8), count), cols] * rows[0:1, cols]
        for i in range(1, 4):
            total = total + m["p"][i, pl.ds(pl.multiple_of(at, 8), count), cols] * rows[i : i + 1, cols]
        return total

    for d in range(1, max(NX, NY) + 1):
        if d <= NX:
            a = lax.rem(place.x + d, NX)
            for h in range(2):
                u.m["pa"][h, a] = weighted(a * per, per, slice(2 * h * Q, (2 * h + 1) * Q))
            u.core_send("a", a)
        if d <= NY:
            a = lax.rem(place.y + d, NY)
            for h in range(2):
                for x in range(NX):
                    u.m["pb"][h, a, x * NZ * 8 : (x + 1) * NZ * 8] = weighted(
                        x * per + a * NZ * 8, NZ * 8, slice((2 * h + 1) * Q, (2 * h + 2) * Q)
                    )
            u.core_send("b", a)

    copy_f.wait()
    f.stage1(jnp.concatenate([m["f8"][0], m["f8"][1]], axis=0))
    u.stage1()

    def transpose(step, carry):
        i, x = step // NX, lax.rem(step, NX)
        hi, lo = split(m["t"][i, x].reshape(per, K).T)
        cols = pl.ds(pl.multiple_of(x * per, per), per)
        m["tt_hi"][i, :, cols] = hi
        m["tt_lo"][i, :, cols] = lo
        return carry

    f.stage2()
    lax.fori_loop(0, 2 * NX, transpose, 0)
    u.stage2()
    f.stage3()
    lax.fori_loop(2 * NX, 4 * NX, transpose, 0)
    u.stage3()
    f.stage4()
    f.finish()
    f.assemble(m["s3"], m["st"])
    gram_of(m["st"], m["s3"], J, m["gram_a"], m["cross"])
    inverse = set_gram(m["gram_a"][...] * m["gram_c"][...], m["gx"])
    own = m["second"][place.x, place.y, place.z]
    new_second = update(own, u.finish(), m["gx"], inverse)
    out_second[...] = jnp.where(place.core == 0, new_second[0:4], new_second[4:8])

    g.stage1(new_second)
    g.stage2()
    g.stage3()
    g.stage4()
    g.finish()
    g.assemble(m["s3"], m["st"])

    total = None
    for i in range(4):
        hi, lo = m["tt_hi"][i], m["tt_lo"][i]
        q = mm(jnp.concatenate([hi, hi, lo], axis=1), m["s3"][...]) * rows[i : i + 1, :]
        if i == 0:
            m["q3"][...] = q
        else:
            m["q3"][...] += q
    low = lax.broadcasted_iota(jnp.int32, (8, Q), 0) < 4
    half = NZ // 2 * 8
    for y in range(NY):
        for zp in range(NZ // 2):
            base = (y * NZ + 2 * zp) * NX * 4
            for h in range(2):
                for part in range(2):
                    cols = slice((2 * h + part) * Q, (2 * h + part + 1) * Q)
                    for xp in range(NX // 2):
                        even = m["q3"][base + xp * 8 : base + xp * 8 + 8, cols]
                        odd = m["q3"][base + NX * 4 + xp * 8 : base + NX * 4 + xp * 8 + 8, cols]
                        lower = jnp.where(low, even, pltpu.roll(odd, 4, 0))
                        upper = jnp.where(low, pltpu.roll(even, 4, 0), odd)
                        for k, block in enumerate((lower, upper)):
                            x = 2 * xp + k
                            if part == 0:
                                v.m["pa"][h, x, y * half + zp * 8 : y * half + zp * 8 + 8] = block
                            else:
                                v.m["pb"][h, y, x * half + zp * 8 : x * half + zp * 8 + 8] = block
    for d in range(1, max(NX, NY) + 1):
        if d <= NX:
            v.core_send("a", lax.rem(place.x + d, NX))
        if d <= NY:
            v.core_send("b", lax.rem(place.y + d, NY))
    v.stage1()
    gram_of(m["st"], m["s3"], J, m["gram_b"], m["cross"])
    inverse = set_gram(m["gram_a"][...] * m["gram_b"][...], m["gx"])
    v.stage2()
    v.stage3()

    block = (place.y * NZ + place.z // 2 * 2) * (NX // 2) + place.x // 2
    even = m["third"][pl.ds(pl.multiple_of(block * 8, 8), 8), :]
    odd = m["third"][pl.ds(pl.multiple_of((block + NX // 2) * 8, 8), 8), :]
    low = lax.broadcasted_iota(jnp.int32, (8, R), 0) < 4
    lower = jnp.where(low, even, pltpu.roll(odd, 4, 0))
    upper = jnp.where(low, pltpu.roll(even, 4, 0), odd)
    own = jnp.where(lax.rem(place.x, 2) == 0, lower, upper)
    new_third = update(own, v.finish(), m["gx"], inverse)
    at = lax.rem(place.z, 2) * 4 + place.core * 2
    index = lax.broadcasted_iota(jnp.int32, (8, R), 0)
    out_third[...] = jnp.concatenate(
        [jnp.sum(jnp.where(index == at + k, new_third, 0.0), axis=0, keepdims=True) for k in range(2)], axis=0
    )


def sweep(devices, tensor, first, second, third):
    own, J, K = tensor.shape
    R = third.shape[1]
    shape = Shape(devices, K, R)
    NX, NY, NZ = shape.NX, shape.NY, shape.NZ
    scratch = shape.scratch()
    vmem = pl.BlockSpec(memory_space=pltpu.VMEM)
    hbm = pl.BlockSpec(memory_space=pl.ANY)
    return pl.pallas_call(
        functools.partial(kernel, shape, tuple(scratch)),
        out_shape=(
            jax.ShapeDtypeStruct((4, R), F32),
            jax.ShapeDtypeStruct((4, R), F32),
            jax.ShapeDtypeStruct((2, R), F32),
        ),
        in_specs=[hbm, vmem, hbm, hbm],
        out_specs=(vmem, vmem, vmem),
        scratch_shapes=list(scratch.values()),
        compiler_params=pltpu.CompilerParams(collective_id=0, has_side_effects=True, vmem_limit_bytes=62 * 2**20),
    )(tensor.reshape(own, NY, NZ, NX, 8, K), first, second.reshape(NY, NZ, NX, 8, R), third)


def solution(mesh):
    in_specs = (P("slab", None, None), P("slab", None), P(), P())
    out_specs = (P("slab", None), P("slab", None), P("slab", None))
    body = functools.partial(sweep, mesh.shape["slab"])
    return jax.shard_map(body, mesh=mesh, in_specs=in_specs, out_specs=out_specs, check_vma=False)
```

```python
import functools

import jax
import jax.numpy as jnp
from jax import lax
from jax.experimental import pallas as pl
from jax.experimental.pallas import tpu as pltpu
from jax.sharding import PartitionSpec as P

F32 = jnp.float32
BF16 = jnp.bfloat16
MESH = pl.DeviceIdType.MESH
GRIDS = {256: (4, 4, 8), 16: (2, 2, 2)}


def mm(a, b):
    return lax.dot_general(a, b, (((1,), (0,)), ((), ())), preferred_element_type=F32)


def split(v):
    hi = v.astype(BF16)
    return hi, (v - hi.astype(F32)).astype(BF16)


def sum8(v):
    rows, cols = v.shape
    return jnp.sum(v.reshape(rows // 8, 8, cols), axis=0)


class Shape:
    def __init__(self, devices, K, R):
        self.NX, self.NY, self.NZ = GRIDS[devices]
        self.J = 8 * self.NX * self.NY * self.NZ
        self.K, self.R = K, R
        self.Q = R // 4

    def reduce_scratch(self, tag, blocks):
        NX, NY, NZ, Q = self.NX, self.NY, self.NZ, self.Q
        ra, rb, zb = NY * blocks * 8, NX * blocks * 8, blocks * 8
        dma = pltpu.SemaphoreType.DMA
        out = {
            "pa": pltpu.VMEM((2, NX, ra, Q), F32),
            "pb": pltpu.VMEM((2, NY, rb, Q), F32),
            "ca": pltpu.VMEM((NX, ra, Q), F32),
            "cb": pltpu.VMEM((NY, rb, Q), F32),
            "sa": pltpu.VMEM((NX, ra, Q), F32),
            "sb": pltpu.VMEM((NY, rb, Q), F32),
            "r1a": pltpu.VMEM((NX - 1, ra, Q), F32),
            "r1b": pltpu.VMEM((NY - 1, rb, Q), F32),
            "s2a": pltpu.VMEM((NY, zb, Q), F32),
            "s2b": pltpu.VMEM((NX, zb, Q), F32),
            "r2a": pltpu.VMEM((NY - 1, zb, Q), F32),
            "r2b": pltpu.VMEM((NX - 1, zb, Q), F32),
            "zs": pltpu.VMEM((blocks, 16, Q), F32),
            "rz": pltpu.VMEM((2, NZ, 16, Q), F32),
            "mh": pltpu.VMEM((2, 16, Q), F32),
        }
        for name, count in (("c", NX + NY), ("1a", NX - 1), ("1b", NY - 1), ("2a", NY - 1), ("2b", NX - 1), ("z", 2 * NZ)):
            out["send_" + name] = dma((count,))
            out["recv_" + name] = dma((count,))
        return {tag + k: v for k, v in out.items()}

    def gather_scratch(self, tag):
        NX, NY, NZ, Q = self.NX, self.NY, self.NZ, self.Q
        dma = pltpu.SemaphoreType.DMA
        out = {
            "zg": pltpu.VMEM((NZ, 16, Q), F32),
            "ga": pltpu.VMEM((2, NX, NY, NZ * 8, Q), F32),
            "gb": pltpu.VMEM((2, NY, NX, NZ * 8, Q), F32),
        }
        for name, count in (("z", NZ - 1), ("2a", NY - 1), ("2b", NX - 1), ("3a", NX - 1), ("3b", NY - 1), ("c", NX + NY)):
            out["send_" + name] = dma((count,))
            out["recv_" + name] = dma((count,))
        return {tag + k: v for k, v in out.items()}

    def scratch(self):
        J, K, R, NX, NY, NZ, Q = self.J, self.K, self.R, self.NX, self.NY, self.NZ, self.Q
        dma = pltpu.SemaphoreType.DMA
        out = {
            "t": pltpu.VMEM((4, NX, NY, NZ, 8, K), F32),
            "second": pltpu.VMEM((NX, NY, NZ, 8, R), F32),
            "third": pltpu.VMEM((K, R), F32),
            "p": pltpu.VMEM((4, J, R), F32),
            "b3": pltpu.VMEM((3 * K, R), BF16),
            "ta_hi": pltpu.VMEM((4, NX, K, J // NX), BF16),
            "ta_lo": pltpu.VMEM((4, NX, K, J // NX), BF16),
            "tb_hi": pltpu.VMEM((4, NY, K, J // NY), BF16),
            "tb_lo": pltpu.VMEM((4, NY, K, J // NY), BF16),
            "w": pltpu.VMEM((3 * J // min(NX, NY), 2 * Q), BF16),
            "s3": pltpu.VMEM((3 * J, R), BF16),
            "st": pltpu.VMEM((R, J), BF16),
            "gram_c": pltpu.VMEM((R, R), F32),
            "gram_a": pltpu.VMEM((R, R), F32),
            "gram_b": pltpu.VMEM((R, R), F32),
            "cross": pltpu.VMEM((R, R), F32),
            "qa": pltpu.VMEM((K, 2 * Q), F32),
            "qb": pltpu.VMEM((K, 2 * Q), F32),
            "gx": pltpu.VMEM((R, 2 * R), BF16),
            "fs": pltpu.VMEM((4, 8, R), F32),
            "load_t": dma((4 * NX,)),
            "load_s": dma((NX,)),
            "load_b": dma((1,)),
        }
        out.update(self.reduce_scratch("u_", NZ))
        out.update(self.reduce_scratch("v_", NZ // 2))
        out.update(self.gather_scratch("f_"))
        out.update(self.gather_scratch("g_"))
        return out


class Place:
    def __init__(self, shape):
        self.shape = shape
        me = lax.axis_index("slab")
        self.core = lax.rem(me, 2)
        self.x = lax.rem(me // 2, shape.NX)
        self.z = lax.rem(me // (2 * shape.NX), shape.NZ)
        self.y = me // (2 * shape.NX * shape.NZ)

    def device(self, dx=0, dy=0, dz=0, dc=0):
        s = self.shape
        x, y, z = lax.rem(self.x + dx, s.NX), lax.rem(self.y + dy, s.NY), lax.rem(self.z + dz, s.NZ)
        core = lax.rem(self.core + dc, 2)
        return ((y * s.NZ + z) * s.NX + x) * 2 + core

    def partners(self):
        s = self.shape
        return (
            [self.device(dx=d) for d in range(1, s.NX)]
            + [self.device(dy=d) for d in range(1, s.NY)]
            + [self.device(dz=d) for d in range(1, s.NZ)]
            + [self.device(dc=1)]
        )


def remote(src, dst, send, recv, device):
    return pltpu.make_async_remote_copy(src, dst, send, recv, device_id=(device,), device_id_type=MESH)


class Reduce:
    def __init__(self, m, tag, place, blocks):
        self.m = {k[len(tag):]: v for k, v in m.items() if k.startswith(tag)}
        self.place, self.blocks, self.sends = place, blocks, []

    def start(self, src, dst, sem, k, device):
        copy = remote(src, dst, self.m["send_" + sem].at[k], self.m["recv_" + sem].at[k], device)
        copy.start()
        self.sends.append(copy)

    def wait(self, dst, sem, k):
        remote(dst, dst, self.m["send_" + sem].at[k], self.m["recv_" + sem].at[k], self.place.device()).wait_recv()

    def core_send(self, part, a):
        m, place = self.m, self.place
        k = a if part == "a" else place.shape.NX + a
        self.start(m["p" + part].at[0, a], m["c" + part].at[a], "c", k, place.device(dc=1))

    def stage1(self):
        m, place, s = self.m, self.place, self.place.shape
        for d in range(1, max(s.NX, s.NY) + 1):
            for part, n, at in (("a", s.NX, place.x), ("b", s.NY, place.y)):
                if d > n:
                    continue
                a = lax.rem(at + d, n)
                self.wait(m["c" + part].at[a], "c", a if part == "a" else s.NX + a)
                m["s" + part][a] = m["p" + part][1, a] + m["c" + part][a]
                if d < n:
                    to = place.device(dx=d) if part == "a" else place.device(dy=d)
                    self.start(m["s" + part].at[a], m["r1" + part].at[d - 1], "1" + part, d - 1, to)

    def stage2(self):
        m, place, s = self.m, self.place, self.place.shape
        zb = self.blocks * 8
        for part, n1, at1, n2, at2 in (("a", s.NX, place.x, s.NY, place.y), ("b", s.NY, place.y, s.NX, place.x)):
            for d in range(n1 - 1):
                self.wait(m["r1" + part].at[d], "1" + part, d)
            for e in range(1, n2 + 1):
                b = lax.rem(at2 + e, n2)
                rows = pl.ds(pl.multiple_of(b * zb, 8), zb)
                total = m["s" + part][at1, rows]
                for d in range(n1 - 1):
                    total = total + m["r1" + part][d, rows]
                m["s2" + part][b] = total
                if e < n2:
                    to = place.device(dy=e) if part == "a" else place.device(dx=e)
                    self.start(m["s2" + part].at[b], m["r2" + part].at[e - 1], "2" + part, e - 1, to)

    def stage3(self):
        m, place, s = self.m, self.place, self.place.shape
        for half, (part, n2, at2) in enumerate((("a", s.NY, place.y), ("b", s.NX, place.x))):
            for e in range(n2 - 1):
                self.wait(m["r2" + part].at[e], "2" + part, e)
            total = m["s2" + part][at2]
            for e in range(n2 - 1):
                total = total + m["r2" + part][e]
            m["zs"][:, half * 8 : half * 8 + 8] = total.reshape(self.blocks, 8, s.Q)
        per = s.NZ // self.blocks
        for d in range(1, s.NZ):
            block = lax.rem(place.z + d, s.NZ) // per
            self.start(m["zs"].at[block], m["rz"].at[place.core, d], "z", d, place.device(dz=d))
            self.start(m["zs"].at[block], m["rz"].at[place.core, d], "z", s.NZ + d, place.device(dz=d, dc=1))
        self.start(m["zs"].at[place.z // per], m["rz"].at[place.core, 0], "z", s.NZ, place.device(dc=1))

    def finish(self):
        m, place, s = self.m, self.place, self.place.shape
        per = s.NZ // self.blocks
        own, other = m["zs"][place.z // per], None
        for d in range(s.NZ):
            if d > 0:
                self.wait(m["rz"].at[place.core, d], "z", d)
                own = own + m["rz"][place.core, d]
            self.wait(m["rz"].at[1 - place.core, d], "z", s.NZ + d)
            piece = m["rz"][1 - place.core, d]
            other = piece if other is None else other + piece
        m["mh"][place.core] = own
        m["mh"][1 - place.core] = other
        out = jnp.concatenate([m["mh"][h, q * 8 : q * 8 + 8] for h in range(2) for q in range(2)], axis=1)
        for copy in self.sends:
            copy.wait_send()
        return out


class Gather:
    def __init__(self, m, tag, place):
        self.m = {k[len(tag):]: v for k, v in m.items() if k.startswith(tag)}
        self.place, self.sends = place, []

    start = Reduce.start
    wait = Reduce.wait

    def stage1(self, block):
        m, place, s = self.m, self.place, self.place.shape
        m["zg"][place.z] = block
        for d in range(1, s.NZ):
            self.start(m["zg"].at[place.z], m["zg"].at[place.z], "z", d - 1, place.device(dz=d))

    def stage2(self):
        m, place, s = self.m, self.place, self.place.shape
        for d in range(1, s.NZ):
            self.wait(m["zg"].at[lax.rem(place.z + s.NZ - d, s.NZ)], "z", d - 1)
        m["ga"][place.core, place.x, place.y] = m["zg"][:, 0:8].reshape(s.NZ * 8, s.Q)
        m["gb"][place.core, place.y, place.x] = m["zg"][:, 8:16].reshape(s.NZ * 8, s.Q)
        for e in range(1, s.NY):
            ref = m["ga"].at[place.core, place.x, place.y]
            self.start(ref, ref, "2a", e - 1, place.device(dy=e))
        for e in range(1, s.NX):
            ref = m["gb"].at[place.core, place.y, place.x]
            self.start(ref, ref, "2b", e - 1, place.device(dx=e))

    def stage3(self):
        m, place, s = self.m, self.place, self.place.shape
        for e in range(1, s.NY):
            self.wait(m["ga"].at[place.core, place.x, lax.rem(place.y + s.NY - e, s.NY)], "2a", e - 1)
        for e in range(1, s.NX):
            self.wait(m["gb"].at[place.core, place.y, lax.rem(place.x + s.NX - e, s.NX)], "2b", e - 1)
        ref, other = m["ga"].at[place.core, place.x], m["gb"].at[place.core, place.y]
        self.start(ref, ref, "c", 0, place.device(dc=1))
        self.start(other, other, "c", s.NX, place.device(dc=1))
        for d in {2: (1,), 4: (1, 3, 2)}[max(s.NX, s.NY)]:
            if d < s.NX:
                self.start(ref, ref, "3a", d - 1, place.device(dx=d))
            if d < s.NY:
                self.start(other, other, "3b", d - 1, place.device(dy=d))

    def forward(self, part, d):
        m, place, s = self.m, self.place, self.place.shape
        if part == 0:
            ref = m["ga"].at[place.core, lax.rem(place.x + s.NX - d, s.NX)]
            self.wait(ref, "3a", d - 1)
            self.start(ref, ref, "c", d, place.device(dc=1))
        else:
            ref = m["gb"].at[place.core, lax.rem(place.y + s.NY - d, s.NY)]
            self.wait(ref, "3b", d - 1)
            self.start(ref, ref, "c", s.NX + d, place.device(dc=1))

    def arrive(self, part, d):
        m, place, s = self.m, self.place, self.place.shape
        if part == 0:
            self.wait(m["ga"].at[1 - place.core, lax.rem(place.x + s.NX - d, s.NX)], "c", d)
        else:
            self.wait(m["gb"].at[1 - place.core, lax.rem(place.y + s.NY - d, s.NY)], "c", s.NX + d)

    def piece(self, part, d):
        m, place, s = self.m, self.place, self.place.shape
        self.arrive(part, d)
        if part == 0:
            ref, at, rows = m["ga"], lax.rem(place.x + s.NX - d, s.NX), s.J // s.NX
        else:
            ref, at, rows = m["gb"], lax.rem(place.y + s.NY - d, s.NY), s.J // s.NY
        return jnp.concatenate([ref[h, at].reshape(rows, s.Q) for h in range(2)], axis=1)

    def drain(self):
        for copy in self.sends:
            copy.wait_send()

    def finish(self):
        s = self.place.shape
        for d in range(1, max(s.NX, s.NY)):
            for part, n in ((0, s.NX), (1, s.NY)):
                if d < n:
                    self.forward(part, d)
        for part, n in ((0, s.NX), (1, s.NY)):
            for d in range(n):
                self.arrive(part, d)
        self.drain()

    def assemble(self, s3, st):
        m, s = self.m, self.place.shape
        J, Q, rows = s.J, s.Q, s.NZ * 8
        per = s.NY * rows

        def step(x, carry):
            for h in range(2):
                for part in range(2):
                    cols = slice((h * 2 + part) * Q, (h * 2 + part + 1) * Q)
                    if part == 0:
                        v = m["ga"][h, x].reshape(per, Q)
                    else:
                        v = jnp.concatenate([m["gb"][h, y, x] for y in range(s.NY)], axis=0)
                    hi, lo = split(v)
                    at = pl.multiple_of(x * per, per)
                    s3[pl.ds(at, per), cols] = hi
                    s3[pl.ds(J + at, per), cols] = lo
                    s3[pl.ds(2 * J + at, per), cols] = hi
                    st[cols, pl.ds(at, per)] = v.T.astype(BF16)
            return carry

        for x in range(s.NX):
            step(x, 0)

    def assemble_first(self, s3, st):
        m, s = self.m, self.place.shape
        J, Q, per = s.J, s.Q, s.NY * s.NZ * 8
        count = per // 2
        top = lax.broadcasted_iota(jnp.int32, (per // 16, 8, Q), 1) < 4
        for h in range(2):
            for x in range(s.NX):
                at = (h * s.NX + x) * count
                for part in range(2):
                    if part == 0:
                        v = m["ga"][h, x].reshape(per, Q)
                    else:
                        v = jnp.concatenate([m["gb"][h, y, x] for y in range(s.NY)], axis=0)
                    v = v.reshape(per // 16, 2, 8, Q)
                    even, odd = v[:, 0], v[:, 1]
                    lower = jnp.where(top, even, pltpu.roll(odd, 4, 1)).reshape(count, Q)
                    upper = jnp.where(top, pltpu.roll(even, 4, 1), odd).reshape(count, Q)
                    for k, v in enumerate((lower, upper)):
                        cols = slice((part * 2 + k) * Q, (part * 2 + k + 1) * Q)
                        hi, lo = split(v)
                        s3[at : at + count, cols] = hi
                        s3[J + at : J + at + count, cols] = lo
                        st[cols, at : at + count] = v.T.astype(BF16)


def gram_of(st, s3, rows, out, cross):
    hi, lo = s3[0:rows, :], s3[rows : 2 * rows, :]
    t = st[:, 0:rows]
    cross[...] = mm(t, lo)
    out[...] = mm(t, hi)
    out[...] = out[...] + cross[...] + cross[...].T


def load_factor(get, rows, block, s3, st):
    for at in range(0, rows, block):
        v = get(at)
        hi, lo = split(v)
        s3[at : at + block, :] = hi
        s3[rows + at : rows + at + block, :] = lo
        s3[2 * rows + at : 2 * rows + at + block, :] = hi
        st[:, at : at + block] = v.T.astype(BF16)


def set_gram(g, gx):
    hi, lo = split(g)
    R = g.shape[0]
    gx[:, 0:R] = hi
    gx[:, R : 2 * R] = lo
    return 1.0 / jnp.max(jnp.sum(g, axis=0, keepdims=True), axis=1, keepdims=True)


def product_of(rows, gx):
    n, R = rows.shape
    hi = rows.astype(BF16).astype(F32)
    both = jnp.concatenate([hi, rows - hi], axis=0).astype(BF16)
    product = mm(both, gx[...])
    product = product[:n] + product[n:]
    return product[:, :R] + product[:, R:]


def update(rows, product, sums, gx, inverse):
    previous = extrapolated = updated = rows
    for turn in range(4):
        if turn > 0:
            product = product_of(extrapolated, gx)
        updated = jnp.maximum(extrapolated - (product - sums) * inverse, 0.0)
        if turn < 3:
            extrapolated = updated + turn / (turn + 3.0) * (updated - previous)
            previous = updated
    return updated


def kernel(shape, names, tensor, first, second, third, out, *refs):
    m = dict(zip(names, refs))
    s, place = shape, Place(shape)
    J, K, R, NX, NY, NZ, Q = s.J, s.K, s.R, s.NX, s.NY, s.NZ, s.Q
    per = NY * NZ * 8

    load_b = pltpu.make_async_copy(third, m["third"], m["load_b"].at[0])
    load_b.start()

    def load_t(i, x):
        return pltpu.make_async_copy(tensor.at[i, :, :, x], m["t"].at[i, x], m["load_t"].at[i * NX + x])

    def load_s(x):
        return pltpu.make_async_copy(second.at[:, :, x], m["second"].at[x], m["load_s"].at[x])

    for x in range(NX):
        load_t(0, x).start()
    for x in range(NX):
        load_s(x).start()
    for i in range(1, 4):
        for x in range(NX):
            load_t(i, x).start()

    barrier = pltpu.get_barrier_semaphore()
    partners = place.partners()
    for device in partners:
        pl.semaphore_signal(barrier, inc=1, device_id=(device,), device_id_type=MESH)

    load_b.wait()
    load_factor(lambda at: m["third"][at : at + K // 4, :], K, K // 4, m["b3"], m["st"])
    gram_of(m["st"], m["b3"], K, m["gram_c"], m["cross"])
    for x in range(NX):
        load_s(x).wait()

    for i in range(4):
        for x in range(NX):
            load_t(i, x).wait()
        hi, lo = split(m["t"][i].reshape(J, K))
        p = mm(jnp.concatenate([hi, hi, lo], axis=1), m["b3"][...])
        m["p"][i] = p
        m["fs"][i] = sum8(p * m["second"][...].reshape(J, R))

    load_factor(lambda at: m["second"][at // per].reshape(per, R), J, per, m["s3"], m["st"])
    gram_of(m["st"], m["s3"], J, m["gram_b"], m["cross"])
    inverse = set_gram(m["gram_b"][...] * m["gram_c"][...], m["gx"])
    sums = jnp.concatenate([jnp.sum(m["fs"][i], axis=0, keepdims=True) for i in range(4)] * 2, axis=0)
    start = first[...]
    start = jnp.concatenate([start, start], axis=0)
    rows = update(start, product_of(start, m["gx"]), sums, m["gx"], inverse)
    new_first = rows[0:4]
    out[0:4, :] = new_first

    pl.semaphore_wait(barrier, len(partners))
    u = Reduce(m, "u_", place, NZ)
    v = Reduce(m, "v_", place, NZ // 2)
    f = Gather(m, "f_", place)
    g = Gather(m, "g_", place)

    top = lax.broadcasted_iota(jnp.int32, (8, Q), 0) < 4
    quarters = [rows[:, q * Q : (q + 1) * Q] for q in range(4)]
    f.stage1(jnp.concatenate([jnp.where(top, quarters[q], quarters[q + 1]) for q in (0, 2)], axis=0))

    halves = (rows[:, : 2 * Q], rows[:, 2 * Q :])
    weights = (jnp.where(place.core == 0, halves[1], halves[0]), jnp.where(place.core == 0, halves[0], halves[1]))

    def weighted(at, count, own, part):
        half = place.core if own else 1 - place.core
        cols = pl.ds(pl.multiple_of((2 * half + part) * Q, Q), Q)
        w = weights[own][:, part * Q : (part + 1) * Q]
        total = m["p"][0, pl.ds(pl.multiple_of(at, 8), count), cols] * w[0:1]
        for i in range(1, 4):
            total = total + m["p"][i, pl.ds(pl.multiple_of(at, 8), count), cols] * w[i : i + 1]
        return total

    for own in (0, 1):
        for d in range(1, max(NX, NY) + 1):
            if d <= NX:
                a = lax.rem(place.x + d, NX)
                u.m["pa"][own, a] = weighted(a * per, per, own, 0)
                if not own:
                    u.core_send("a", a)
            if d <= NY:
                a = lax.rem(place.y + d, NY)
                for x in range(NX):
                    u.m["pb"][own, a, x * NZ * 8 : (x + 1) * NZ * 8] = weighted(x * per + a * NZ * 8, NZ * 8, own, 1)
                if not own:
                    u.core_send("b", a)
    u.stage1()

    def transpose_a(step, carry):
        i, x = step // NX, lax.rem(step, NX)
        hi, lo = split(m["t"][i, x].reshape(per, K).T)
        m["ta_hi"][i, x] = hi
        m["ta_lo"][i, x] = lo
        return carry

    def transpose_b(step, carry):
        i, y = step // NY, lax.rem(step, NY)
        hi, lo = split(m["t"][i, :, y].reshape(NX * NZ * 8, K).T)
        m["tb_hi"][i, y] = hi
        m["tb_lo"][i, y] = lo
        return carry

    f.stage2()
    lax.fori_loop(0, 4 * NX, transpose_a, 0)
    u.stage2()
    f.stage3()
    lax.fori_loop(0, 4 * NY, transpose_b, 0)
    u.stage3()
    f.finish()
    f.assemble_first(m["s3"], m["st"])
    gram_of(m["st"], m["s3"], J, m["gram_a"], m["cross"])
    inverse = set_gram(m["gram_a"][...] * m["gram_c"][...], m["gx"])
    own = m["second"][place.x, place.y, place.z]
    ahead = product_of(own, m["gx"])
    new_second = update(own, ahead, u.finish(), m["gx"], inverse)
    out[4:8, :] = jnp.where(place.core == 0, new_second[0:4], new_second[4:8])

    own = jnp.where(place.core == 0, new_second[:, : 2 * Q], new_second[:, 2 * Q :])
    g.stage1(jnp.concatenate([own[:, :Q], own[:, Q:]], axis=0))
    g.stage2()
    g.stage3()
    half = NZ // 2 * 8
    low = lax.broadcasted_iota(jnp.int32, (8, Q), 0) < 4
    weight = [
        [jnp.concatenate([rows[i : i + 1, c * Q : (c + 1) * Q] for c in (part, 2 + part)], axis=1) for i in range(4)]
        for part in range(2)
    ]

    def third_piece(part, d, first_piece):
        n, at, q = ((NX, place.x, m["qa"]), (NY, place.y, m["qb"]))[part]
        t_hi, t_lo = ((m["ta_hi"], m["ta_lo"]), (m["tb_hi"], m["tb_lo"]))[part]
        count = J // n
        piece = g.piece(part, d)
        hi, lo = split(piece)
        m["w"][0:count] = hi
        m["w"][count : 2 * count] = lo
        m["w"][2 * count : 3 * count] = hi
        at = lax.rem(at + n - d, n)
        for i in range(4):
            left = jnp.concatenate([t_hi[i, at], t_hi[i, at], t_lo[i, at]], axis=1)
            product = mm(left, m["w"][0 : 3 * count]) * weight[part][i]
            if first_piece and i == 0:
                q[...] = product
            else:
                q[...] += product

    def third_place(part, own):
        q = (m["qa"], m["qb"])[part]
        cols = pl.ds(pl.multiple_of((place.core if own else 1 - place.core) * Q, Q), Q)
        for y in range(NY):
            for zp in range(NZ // 2):
                base = (y * NZ + 2 * zp) * NX * 4
                for xp in range(NX // 2):
                    even = q[base + xp * 8 : base + xp * 8 + 8, cols]
                    odd = q[base + NX * 4 + xp * 8 : base + NX * 4 + xp * 8 + 8, cols]
                    lower = jnp.where(low, even, pltpu.roll(odd, 4, 0))
                    upper = jnp.where(low, pltpu.roll(even, 4, 0), odd)
                    for k, block in enumerate((lower, upper)):
                        x = 2 * xp + k
                        if part == 0:
                            v.m["pa"][own, x, y * half + zp * 8 : y * half + zp * 8 + 8] = block
                        else:
                            v.m["pb"][own, y, x * half + zp * 8 : x * half + zp * 8 + 8] = block
        if not own:
            n, at, name = ((NX, place.x, "a"), (NY, place.y, "b"))[part]
            for d in range(1, n + 1):
                v.core_send(name, lax.rem(at + d, n))

    third_piece(0, 0, True)
    third_piece(1, 0, True)
    order = {2: (1,), 4: (1, 3, 2)}
    g.forward(0, 1)
    g.forward(1, 1)
    later = order[NX][1:]
    done = [1]
    for d in later:
        g.forward(0, d)
        g.forward(1, d)
        if d != later[-1]:
            third_piece(0, done[-1], False)
            third_piece(1, done[-1], False)
            done.append(d)
    last = [d for d in order[NX] if d not in done[:-1]]
    for part in range(2):
        for d in last:
            third_piece(part, d, False)
        third_place(part, 0)
    third_place(0, 1)
    third_place(1, 1)
    v.stage1()
    g.drain()
    g.assemble(m["s3"], m["st"])
    gram_of(m["st"], m["s3"], J, m["gram_b"], m["cross"])
    inverse = set_gram(m["gram_a"][...] * m["gram_b"][...], m["gx"])
    v.stage2()
    v.stage3()

    block = (place.y * NZ + place.z // 2 * 2) * (NX // 2) + place.x // 2
    even = m["third"][pl.ds(pl.multiple_of(block * 8, 8), 8), :]
    odd = m["third"][pl.ds(pl.multiple_of((block + NX // 2) * 8, 8), 8), :]
    low = lax.broadcasted_iota(jnp.int32, (8, R), 0) < 4
    lower = jnp.where(low, even, pltpu.roll(odd, 4, 0))
    upper = jnp.where(low, pltpu.roll(even, 4, 0), odd)
    own = jnp.where(lax.rem(place.x, 2) == 0, lower, upper)
    ahead = product_of(own, m["gx"])
    new_third = update(own, ahead, v.finish(), m["gx"], inverse)
    at = lax.rem(place.z, 2) * 4 + place.core * 2
    index = lax.broadcasted_iota(jnp.int32, (8, R), 0)
    out[8:10, :] = jnp.concatenate(
        [jnp.sum(jnp.where(index == at + k, new_third, 0.0), axis=0, keepdims=True) for k in range(2)], axis=0
    )


def hand_out(rows, out_first, out_second, out_third):
    out_first[...] = rows[0:4, :]
    out_second[...] = rows[4:8, :]
    out_third[...] = rows[8:10, :]


def sweep(devices, tensor, first, second, third):
    own, J, K = tensor.shape
    R = third.shape[1]
    shape = Shape(devices, K, R)
    NX, NY, NZ = shape.NX, shape.NY, shape.NZ
    scratch = shape.scratch()
    vmem = pl.BlockSpec(memory_space=pltpu.VMEM)
    hbm = pl.BlockSpec(memory_space=pl.ANY)
    out = pl.pallas_call(
        functools.partial(kernel, shape, tuple(scratch)),
        out_shape=jax.ShapeDtypeStruct((10, R), F32),
        in_specs=[hbm, vmem, hbm, hbm],
        out_specs=vmem,
        scratch_shapes=list(scratch.values()),
        compiler_params=pltpu.CompilerParams(collective_id=0, has_side_effects=True, vmem_limit_bytes=62 * 2**20),
    )(tensor.reshape(own, NY, NZ, NX, 8, K), first, second.reshape(NY, NZ, NX, 8, R), third)
    return pl.pallas_call(
        hand_out,
        out_shape=(
            jax.ShapeDtypeStruct((4, R), F32),
            jax.ShapeDtypeStruct((4, R), F32),
            jax.ShapeDtypeStruct((2, R), F32),
        ),
        in_specs=[vmem],
        out_specs=(vmem, vmem, vmem),
    )(out)


def solution(mesh):
    in_specs = (P("slab", None, None), P("slab", None), P(), P())
    out_specs = (P("slab", None), P("slab", None), P("slab", None))
    body = functools.partial(sweep, mesh.shape["slab"])
    return jax.shard_map(body, mesh=mesh, in_specs=in_specs, out_specs=out_specs, check_vma=False)
```

```python
import functools

import jax
import jax.numpy as jnp
from jax import lax
from jax.experimental import pallas as pl
from jax.experimental.pallas import tpu as pltpu
from jax.sharding import PartitionSpec as P

F32 = jnp.float32
BF16 = jnp.bfloat16
MESH = pl.DeviceIdType.MESH
GRIDS = {256: (4, 4, 8), 16: (2, 2, 2)}


def mm(a, b):
    return lax.dot_general(a, b, (((1,), (0,)), ((), ())), preferred_element_type=F32)


def split(v):
    hi = v.astype(BF16)
    return hi, (v - hi.astype(F32)).astype(BF16)


def sum8(v):
    rows, cols = v.shape
    return jnp.sum(v.reshape(rows // 8, 8, cols), axis=0)


class Shape:
    def __init__(self, devices, K, R):
        self.NX, self.NY, self.NZ = GRIDS[devices]
        self.J = 8 * self.NX * self.NY * self.NZ
        self.K, self.R = K, R
        self.Q = R // 4

    def reduce_scratch(self, tag, blocks):
        NX, NY, NZ, Q = self.NX, self.NY, self.NZ, self.Q
        ra, rb, zb = NY * blocks * 8, NX * blocks * 8, blocks * 8
        dma = pltpu.SemaphoreType.DMA
        out = {
            "pa": pltpu.VMEM((2, NX, ra, Q), F32),
            "pb": pltpu.VMEM((2, NY, rb, Q), F32),
            "ca": pltpu.VMEM((NX, ra, Q), F32),
            "cb": pltpu.VMEM((NY, rb, Q), F32),
            "sa": pltpu.VMEM((NX, ra, Q), F32),
            "sb": pltpu.VMEM((NY, rb, Q), F32),
            "r1a": pltpu.VMEM((NX - 1, ra, Q), F32),
            "r1b": pltpu.VMEM((NY - 1, rb, Q), F32),
            "s2a": pltpu.VMEM((NY, zb, Q), F32),
            "s2b": pltpu.VMEM((NX, zb, Q), F32),
            "r2a": pltpu.VMEM((NY - 1, zb, Q), F32),
            "r2b": pltpu.VMEM((NX - 1, zb, Q), F32),
            "zs": pltpu.VMEM((blocks, 16, Q), F32),
            "rz": pltpu.VMEM((2, NZ, 16, Q), F32),
            "mh": pltpu.VMEM((2, 16, Q), F32),
        }
        for name, count in (("c", NX + NY), ("1a", NX - 1), ("1b", NY - 1), ("la", NX - 1), ("lb", NY - 1), ("2a", NY - 1), ("2b", NX - 1), ("z", 2 * NZ)):
            out["send_" + name] = dma((count,))
            out["recv_" + name] = dma((count,))
        return {tag + k: v for k, v in out.items()}

    def gather_scratch(self, tag):
        NX, NY, NZ, Q = self.NX, self.NY, self.NZ, self.Q
        dma = pltpu.SemaphoreType.DMA
        out = {
            "zg": pltpu.VMEM((NZ, 16, Q), F32),
            "ga": pltpu.VMEM((2, NX, NY, NZ * 8, Q), F32),
            "gb": pltpu.VMEM((2, NY, NX, NZ * 8, Q), F32),
        }
        for name, count in (("z", NZ - 1), ("2a", NY - 1), ("2b", NX - 1), ("3a", NX - 1), ("3b", NY - 1), ("4a", NX - 1), ("4b", NY - 1), ("c", NX + NY)):
            out["send_" + name] = dma((count,))
            out["recv_" + name] = dma((count,))
        return {tag + k: v for k, v in out.items()}

    def scratch(self):
        J, K, R, NX, NY, NZ, Q = self.J, self.K, self.R, self.NX, self.NY, self.NZ, self.Q
        dma = pltpu.SemaphoreType.DMA
        out = {
            "t": pltpu.VMEM((4, NX, NY, NZ, 8, K), F32),
            "second": pltpu.VMEM((NX, NY, NZ, 8, R), F32),
            "third": pltpu.VMEM((K, R), F32),
            "p": pltpu.VMEM((4, J, R), F32),
            "b3": pltpu.VMEM((3 * K, R), BF16),
            "ta_hi": pltpu.VMEM((4, NX, K, J // NX), BF16),
            "ta_lo": pltpu.VMEM((4, NX, K, J // NX), BF16),
            "tb_hi": pltpu.VMEM((4, NY, K, J // NY), BF16),
            "tb_lo": pltpu.VMEM((4, NY, K, J // NY), BF16),
            "w": pltpu.VMEM((3 * J // min(NX, NY), 2 * Q), BF16),
            "s3": pltpu.VMEM((3 * J, R), BF16),
            "st": pltpu.VMEM((R, J), BF16),
            "gram_c": pltpu.VMEM((R, R), F32),
            "gram_a": pltpu.VMEM((R, R), F32),
            "gram_b": pltpu.VMEM((R, R), F32),
            "cross": pltpu.VMEM((R, R), F32),
            "qa": pltpu.VMEM((K, 2 * Q), F32),
            "qb": pltpu.VMEM((K, 2 * Q), F32),
            "gx": pltpu.VMEM((R, 2 * R), BF16),
            "fs": pltpu.VMEM((4, 8, R), F32),
            "load_t": dma((4 * NX,)),
            "load_s": dma((NX,)),
            "load_b": dma((1,)),
        }
        out.update(self.reduce_scratch("u_", NZ))
        out.update(self.reduce_scratch("v_", NZ // 2))
        out.update(self.gather_scratch("f_"))
        out.update(self.gather_scratch("g_"))
        return out


class Place:
    def __init__(self, shape):
        self.shape = shape
        me = lax.axis_index("slab")
        self.core = lax.rem(me, 2)
        self.x = lax.rem(me // 2, shape.NX)
        self.z = lax.rem(me // (2 * shape.NX), shape.NZ)
        self.y = me // (2 * shape.NX * shape.NZ)

    def device(self, dx=0, dy=0, dz=0, dc=0):
        s = self.shape
        x, y, z = lax.rem(self.x + dx, s.NX), lax.rem(self.y + dy, s.NY), lax.rem(self.z + dz, s.NZ)
        core = lax.rem(self.core + dc, 2)
        return ((y * s.NZ + z) * s.NX + x) * 2 + core

    def partners(self):
        s = self.shape
        return (
            [self.device(dx=d) for d in range(1, s.NX)]
            + [self.device(dy=d) for d in range(1, s.NY)]
            + [self.device(dz=d) for d in range(1, s.NZ)]
            + [self.device(dc=1)]
        )


def remote(src, dst, send, recv, device):
    return pltpu.make_async_remote_copy(src, dst, send, recv, device_id=(device,), device_id_type=MESH)


class Reduce:
    def __init__(self, m, tag, place, blocks):
        self.m = {k[len(tag):]: v for k, v in m.items() if k.startswith(tag)}
        self.place, self.blocks, self.sends = place, blocks, []

    def start(self, src, dst, sem, k, device):
        copy = remote(src, dst, self.m["send_" + sem].at[k], self.m["recv_" + sem].at[k], device)
        copy.start()
        self.sends.append(copy)

    def wait(self, dst, sem, k):
        remote(dst, dst, self.m["send_" + sem].at[k], self.m["recv_" + sem].at[k], self.place.device()).wait_recv()

    def core_send(self, part, a):
        m, place = self.m, self.place
        k = a if part == "a" else place.shape.NX + a
        self.start(m["p" + part].at[0, a], m["c" + part].at[a], "c", k, place.device(dc=1))

    def stage1(self):
        m, place, s = self.m, self.place, self.place.shape
        zb = self.blocks * 8
        late = []
        for d in range(1, max(s.NX, s.NY) + 1):
            for part, n, at, n2, at2 in (("a", s.NX, place.x, s.NY, place.y), ("b", s.NY, place.y, s.NX, place.x)):
                if d > n:
                    continue
                a = lax.rem(at + d, n)
                self.wait(m["c" + part].at[a], "c", a if part == "a" else s.NX + a)
                for e in range(n2):
                    rows = pl.ds(pl.multiple_of(lax.rem(at2 + e, n2) * zb, 8), zb)
                    m["s" + part][a, e * zb : (e + 1) * zb] = m["p" + part][1, a, rows] + m["c" + part][a, rows]
                if d < n:
                    to = place.device(dx=d) if part == "a" else place.device(dy=d)
                    rest = pl.ds(zb, (n2 - 1) * zb)
                    self.start(m["s" + part].at[a, rest], m["r1" + part].at[d - 1, rest], "1" + part, d - 1, to)
                    late.append((part, a, d, to))
        for part, a, d, to in late:
            own = pl.ds(0, zb)
            self.start(m["s" + part].at[a, own], m["r1" + part].at[d - 1, own], "l" + part, d - 1, to)

    def stage2(self):
        m, place, s = self.m, self.place, self.place.shape
        zb = self.blocks * 8
        parts = (("a", s.NX, place.x, s.NY), ("b", s.NY, place.y, s.NX))

        def total(part, n1, at1, e):
            rows = slice(e * zb, (e + 1) * zb)
            value = m["s" + part][at1, rows]
            for d in range(n1 - 1):
                value = value + m["r1" + part][d, rows]
            m["s2" + part][e] = value

        for part, n1, at1, n2 in parts:
            for d in range(n1 - 1):
                self.wait(m["r1" + part].at[d, pl.ds(zb, (n2 - 1) * zb)], "1" + part, d)
            for e in range(1, n2):
                total(part, n1, at1, e)
                to = place.device(dy=e) if part == "a" else place.device(dx=e)
                self.start(m["s2" + part].at[e], m["r2" + part].at[e - 1], "2" + part, e - 1, to)

    def stage2_own(self):
        m, place, s = self.m, self.place, self.place.shape
        zb = self.blocks * 8
        for part, n1, at1 in (("a", s.NX, place.x), ("b", s.NY, place.y)):
            for d in range(n1 - 1):
                self.wait(m["r1" + part].at[d, pl.ds(0, zb)], "l" + part, d)
            value = m["s" + part][at1, 0:zb]
            for d in range(n1 - 1):
                value = value + m["r1" + part][d, 0:zb]
            m["s2" + part][0] = value

    def stage3(self):
        m, place, s = self.m, self.place, self.place.shape
        self.stage2_own()
        for half, (part, n2) in enumerate((("a", s.NY), ("b", s.NX))):
            for e in range(n2 - 1):
                self.wait(m["r2" + part].at[e], "2" + part, e)
            total = m["s2" + part][0]
            for e in range(n2 - 1):
                total = total + m["r2" + part][e]
            m["zs"][:, half * 8 : half * 8 + 8] = total.reshape(self.blocks, 8, s.Q)
        per = s.NZ // self.blocks
        for d in range(1, s.NZ):
            block = lax.rem(place.z + d, s.NZ) // per
            self.start(m["zs"].at[block], m["rz"].at[place.core, d], "z", d, place.device(dz=d))
            self.start(m["zs"].at[block], m["rz"].at[place.core, d], "z", s.NZ + d, place.device(dz=d, dc=1))
        self.start(m["zs"].at[place.z // per], m["rz"].at[place.core, 0], "z", s.NZ, place.device(dc=1))

    def finish(self):
        m, place, s = self.m, self.place, self.place.shape
        per = s.NZ // self.blocks
        own, other = m["zs"][place.z // per], None
        for d in range(s.NZ):
            if d > 0:
                self.wait(m["rz"].at[place.core, d], "z", d)
                own = own + m["rz"][place.core, d]
            self.wait(m["rz"].at[1 - place.core, d], "z", s.NZ + d)
            piece = m["rz"][1 - place.core, d]
            other = piece if other is None else other + piece
        m["mh"][place.core] = own
        m["mh"][1 - place.core] = other
        out = jnp.concatenate([m["mh"][h, q * 8 : q * 8 + 8] for h in range(2) for q in range(2)], axis=1)
        for copy in self.sends:
            copy.wait_send()
        return out


class Gather:
    def __init__(self, m, tag, place):
        self.m = {k[len(tag):]: v for k, v in m.items() if k.startswith(tag)}
        self.place, self.sends = place, []

    start = Reduce.start
    wait = Reduce.wait

    def stage1(self, block):
        m, place, s = self.m, self.place, self.place.shape
        m["zg"][place.z] = block
        for d in range(1, s.NZ):
            self.start(m["zg"].at[place.z], m["zg"].at[place.z], "z", d - 1, place.device(dz=d))

    def stage2(self):
        m, place, s = self.m, self.place, self.place.shape
        for d in range(1, s.NZ):
            self.wait(m["zg"].at[lax.rem(place.z + s.NZ - d, s.NZ)], "z", d - 1)
        m["ga"][place.core, place.x, 0] = m["zg"][:, 0:8].reshape(s.NZ * 8, s.Q)
        m["gb"][place.core, place.y, 0] = m["zg"][:, 8:16].reshape(s.NZ * 8, s.Q)
        own_a, own_b = m["ga"].at[place.core, place.x, 0], m["gb"].at[place.core, place.y, 0]
        for e in range(1, max(s.NX, s.NY)):
            if e < s.NY:
                self.start(own_a, m["ga"].at[place.core, place.x, s.NY - e], "2a", e - 1, place.device(dy=e))
            if e < s.NX:
                self.start(own_b, m["gb"].at[place.core, place.y, s.NX - e], "2b", e - 1, place.device(dx=e))
        for e in range(1, max(s.NX, s.NY)):
            if e < s.NX:
                self.start(own_a, own_a, "3a", e - 1, place.device(dx=e))
            if e < s.NY:
                self.start(own_b, own_b, "3b", e - 1, place.device(dy=e))

    def stage3(self):
        m, place, s = self.m, self.place, self.place.shape
        for e in range(1, s.NY):
            self.wait(m["ga"].at[place.core, place.x, s.NY - e], "2a", e - 1)
        for e in range(1, s.NX):
            self.wait(m["gb"].at[place.core, place.y, s.NX - e], "2b", e - 1)
        ref, other = m["ga"].at[place.core, place.x], m["gb"].at[place.core, place.y]
        self.start(ref, ref, "c", 0, place.device(dc=1))
        self.start(other, other, "c", s.NX, place.device(dc=1))
        rest_a = m["ga"].at[place.core, place.x, pl.ds(1, s.NY - 1)]
        rest_b = m["gb"].at[place.core, place.y, pl.ds(1, s.NX - 1)]
        for d in {2: (1,), 4: (1, 3, 2)}[max(s.NX, s.NY)]:
            if d < s.NX:
                self.start(rest_a, rest_a, "4a", d - 1, place.device(dx=d))
            if d < s.NY:
                self.start(rest_b, rest_b, "4b", d - 1, place.device(dy=d))

    def forward(self, part, d):
        m, place, s = self.m, self.place, self.place.shape
        if part == 0:
            ref = m["ga"].at[place.core, lax.rem(place.x + s.NX - d, s.NX)]
            self.wait(ref.at[0], "3a", d - 1)
            self.wait(ref.at[pl.ds(1, s.NY - 1)], "4a", d - 1)
            self.start(ref, ref, "c", d, place.device(dc=1))
        else:
            ref = m["gb"].at[place.core, lax.rem(place.y + s.NY - d, s.NY)]
            self.wait(ref.at[0], "3b", d - 1)
            self.wait(ref.at[pl.ds(1, s.NX - 1)], "4b", d - 1)
            self.start(ref, ref, "c", s.NX + d, place.device(dc=1))

    def arrive(self, part, d):
        m, place, s = self.m, self.place, self.place.shape
        if part == 0:
            self.wait(m["ga"].at[1 - place.core, lax.rem(place.x + s.NX - d, s.NX)], "c", d)
        else:
            self.wait(m["gb"].at[1 - place.core, lax.rem(place.y + s.NY - d, s.NY)], "c", s.NX + d)

    def piece(self, part, d):
        m, place, s = self.m, self.place, self.place.shape
        self.arrive(part, d)
        at = lax.rem(place.x + s.NX - d, s.NX) if part == 0 else lax.rem(place.y + s.NY - d, s.NY)
        return jnp.concatenate([self.rows_a(h, at) if part == 0 else self.rows_b(h, at) for h in range(2)], axis=1)

    def rows_a(self, h, x):
        place, s = self.place, self.place.shape
        return jnp.concatenate([self.m["ga"][h, x, lax.rem(y + s.NY - place.y, s.NY)] for y in range(s.NY)], axis=0)

    def rows_b(self, h, y):
        place, s = self.place, self.place.shape
        return jnp.concatenate([self.m["gb"][h, y, lax.rem(x + s.NX - place.x, s.NX)] for x in range(s.NX)], axis=0)

    def rows_b_of(self, h, x):
        place, s = self.place, self.place.shape
        e = lax.rem(x + s.NX - place.x, s.NX)
        return jnp.concatenate([self.m["gb"][h, y, e] for y in range(s.NY)], axis=0)

    def drain(self):
        for copy in self.sends:
            copy.wait_send()

    def finish(self):
        s = self.place.shape
        for d in range(1, max(s.NX, s.NY)):
            for part, n in ((0, s.NX), (1, s.NY)):
                if d < n:
                    self.forward(part, d)
        for part, n in ((0, s.NX), (1, s.NY)):
            for d in range(n):
                self.arrive(part, d)
        self.drain()

    def assemble(self, s3, st):
        m, s = self.m, self.place.shape
        J, Q, rows = s.J, s.Q, s.NZ * 8
        per = s.NY * rows

        def step(x, carry):
            for h in range(2):
                for part in range(2):
                    cols = slice((h * 2 + part) * Q, (h * 2 + part + 1) * Q)
                    if part == 0:
                        v = self.rows_a(h, x)
                    else:
                        v = self.rows_b_of(h, x)
                    hi, lo = split(v)
                    at = pl.multiple_of(x * per, per)
                    s3[pl.ds(at, per), cols] = hi
                    s3[pl.ds(J + at, per), cols] = lo
                    s3[pl.ds(2 * J + at, per), cols] = hi
                    st[cols, pl.ds(at, per)] = v.T.astype(BF16)
            return carry

        for x in range(s.NX):
            step(x, 0)

    def assemble_first(self, s3, st):
        m, s = self.m, self.place.shape
        J, Q, per = s.J, s.Q, s.NY * s.NZ * 8
        count = per // 2
        top = lax.broadcasted_iota(jnp.int32, (per // 16, 8, Q), 1) < 4
        for h in range(2):
            for x in range(s.NX):
                at = (h * s.NX + x) * count
                for part in range(2):
                    if part == 0:
                        v = self.rows_a(h, x)
                    else:
                        v = self.rows_b_of(h, x)
                    v = v.reshape(per // 16, 2, 8, Q)
                    even, odd = v[:, 0], v[:, 1]
                    lower = jnp.where(top, even, pltpu.roll(odd, 4, 1)).reshape(count, Q)
                    upper = jnp.where(top, pltpu.roll(even, 4, 1), odd).reshape(count, Q)
                    for k, v in enumerate((lower, upper)):
                        cols = slice((part * 2 + k) * Q, (part * 2 + k + 1) * Q)
                        hi, lo = split(v)
                        s3[at : at + count, cols] = hi
                        s3[J + at : J + at + count, cols] = lo
                        st[cols, at : at + count] = v.T.astype(BF16)


def gram_of(st, s3, rows, out, cross):
    hi, lo = s3[0:rows, :], s3[rows : 2 * rows, :]
    t = st[:, 0:rows]
    cross[...] = mm(t, lo)
    out[...] = mm(t, hi)
    out[...] = out[...] + cross[...] + cross[...].T


def load_factor(get, rows, block, s3, st):
    for at in range(0, rows, block):
        v = get(at)
        hi, lo = split(v)
        s3[at : at + block, :] = hi
        s3[rows + at : rows + at + block, :] = lo
        s3[2 * rows + at : 2 * rows + at + block, :] = hi
        st[:, at : at + block] = v.T.astype(BF16)


def set_gram(g, gx):
    hi, lo = split(g)
    R = g.shape[0]
    gx[:, 0:R] = hi
    gx[:, R : 2 * R] = lo
    return 1.0 / jnp.max(jnp.sum(g, axis=0, keepdims=True), axis=1, keepdims=True)


def product_of(rows, gx):
    n, R = rows.shape
    hi = rows.astype(BF16).astype(F32)
    both = jnp.concatenate([hi, rows - hi], axis=0).astype(BF16)
    product = mm(both, gx[...])
    product = product[:n] + product[n:]
    return product[:, :R] + product[:, R:]


def update(rows, product, sums, gx, inverse):
    previous = extrapolated = updated = rows
    for turn in range(4):
        if turn > 0:
            product = product_of(extrapolated, gx)
        updated = jnp.maximum(extrapolated - (product - sums) * inverse, 0.0)
        if turn < 3:
            extrapolated = updated + turn / (turn + 3.0) * (updated - previous)
            previous = updated
    return updated


def kernel(shape, names, tensor, first, second, third, out, *refs):
    m = dict(zip(names, refs))
    s, place = shape, Place(shape)
    J, K, R, NX, NY, NZ, Q = s.J, s.K, s.R, s.NX, s.NY, s.NZ, s.Q
    per = NY * NZ * 8

    load_b = pltpu.make_async_copy(third, m["third"], m["load_b"].at[0])
    load_b.start()

    def load_t(i, x):
        return pltpu.make_async_copy(tensor.at[i, :, :, x], m["t"].at[i, x], m["load_t"].at[i * NX + x])

    def load_s(x):
        return pltpu.make_async_copy(second.at[:, :, x], m["second"].at[x], m["load_s"].at[x])

    for x in range(NX):
        load_t(0, x).start()

    barrier = pltpu.get_barrier_semaphore()
    partners = place.partners()
    for device in partners:
        pl.semaphore_signal(barrier, inc=1, device_id=(device,), device_id_type=MESH)

    load_b.wait()
    for x in range(NX):
        load_s(x).start()
    for x in range(NX):
        load_t(1, x).start()
    load_factor(lambda at: m["third"][at : at + K // 4, :], K, K // 4, m["b3"], m["st"])
    gram_of(m["st"], m["b3"], K, m["gram_c"], m["cross"])
    for i in range(4):
        for x in range(NX):
            load_t(i, x).wait()
        if i < 2:
            for x in range(NX):
                load_t(i + 2, x).start()
        hi, lo = split(m["t"][i].reshape(J, K))
        p = mm(jnp.concatenate([hi, hi, lo], axis=1), m["b3"][...])
        m["p"][i] = p
        if i == 0:
            for x in range(NX):
                load_s(x).wait()
        m["fs"][i] = sum8(p * m["second"][...].reshape(J, R))

    load_factor(lambda at: m["second"][at // per].reshape(per, R), J, per, m["s3"], m["st"])
    gram_of(m["st"], m["s3"], J, m["gram_b"], m["cross"])
    inverse = set_gram(m["gram_b"][...] * m["gram_c"][...], m["gx"])
    sums = jnp.concatenate([jnp.sum(m["fs"][i], axis=0, keepdims=True) for i in range(4)] * 2, axis=0)
    start = first[...]
    start = jnp.concatenate([start, start], axis=0)
    rows = update(start, product_of(start, m["gx"]), sums, m["gx"], inverse)
    new_first = rows[0:4]
    out[0:4, :] = new_first

    pl.semaphore_wait(barrier, len(partners))
    u = Reduce(m, "u_", place, NZ)
    v = Reduce(m, "v_", place, NZ // 2)
    f = Gather(m, "f_", place)
    g = Gather(m, "g_", place)

    top = lax.broadcasted_iota(jnp.int32, (8, Q), 0) < 4
    quarters = [rows[:, q * Q : (q + 1) * Q] for q in range(4)]
    f.stage1(jnp.concatenate([jnp.where(top, quarters[q], quarters[q + 1]) for q in (0, 2)], axis=0))

    halves = (rows[:, : 2 * Q], rows[:, 2 * Q :])
    weights = (jnp.where(place.core == 0, halves[1], halves[0]), jnp.where(place.core == 0, halves[0], halves[1]))

    def weighted(at, count, own, part):
        half = place.core if own else 1 - place.core
        cols = pl.ds(pl.multiple_of((2 * half + part) * Q, Q), Q)
        w = weights[own][:, part * Q : (part + 1) * Q]
        total = m["p"][0, pl.ds(pl.multiple_of(at, 8), count), cols] * w[0:1]
        for i in range(1, 4):
            total = total + m["p"][i, pl.ds(pl.multiple_of(at, 8), count), cols] * w[i : i + 1]
        return total

    for own in (0, 1):
        for d in range(1, max(NX, NY) + 1):
            if d <= NX:
                a = lax.rem(place.x + d, NX)
                u.m["pa"][own, a] = weighted(a * per, per, own, 0)
                if not own:
                    u.core_send("a", a)
            if d <= NY:
                a = lax.rem(place.y + d, NY)
                for x in range(NX):
                    u.m["pb"][own, a, x * NZ * 8 : (x + 1) * NZ * 8] = weighted(x * per + a * NZ * 8, NZ * 8, own, 1)
                if not own:
                    u.core_send("b", a)
    u.stage1()

    def transpose_a(step, carry):
        i, x = step // NX, lax.rem(step, NX)
        hi, lo = split(m["t"][i, x].reshape(per, K).T)
        m["ta_hi"][i, x] = hi
        m["ta_lo"][i, x] = lo
        return carry

    def transpose_b(step, carry):
        i, y = step // NY, lax.rem(step, NY)
        hi, lo = split(m["t"][i, :, y].reshape(NX * NZ * 8, K).T)
        m["tb_hi"][i, y] = hi
        m["tb_lo"][i, y] = lo
        return carry

    f.stage2()
    lax.fori_loop(0, 4 * NX, transpose_a, 0)
    u.stage2()
    f.stage3()
    lax.fori_loop(0, 4 * NY, transpose_b, 0)
    u.stage3()
    f.finish()
    f.assemble_first(m["s3"], m["st"])
    gram_of(m["st"], m["s3"], J, m["gram_a"], m["cross"])
    inverse = set_gram(m["gram_a"][...] * m["gram_c"][...], m["gx"])
    own = m["second"][place.x, place.y, place.z]
    ahead = product_of(own, m["gx"])
    new_second = update(own, ahead, u.finish(), m["gx"], inverse)
    out[4:8, :] = jnp.where(place.core == 0, new_second[0:4], new_second[4:8])

    own = jnp.where(place.core == 0, new_second[:, : 2 * Q], new_second[:, 2 * Q :])
    g.stage1(jnp.concatenate([own[:, :Q], own[:, Q:]], axis=0))
    g.stage2()
    g.stage3()
    half = NZ // 2 * 8
    low = lax.broadcasted_iota(jnp.int32, (8, Q), 0) < 4
    weight = [
        [jnp.concatenate([rows[i : i + 1, c * Q : (c + 1) * Q] for c in (part, 2 + part)], axis=1) for i in range(4)]
        for part in range(2)
    ]

    def third_piece(part, d, first_piece):
        n, at, q = ((NX, place.x, m["qa"]), (NY, place.y, m["qb"]))[part]
        t_hi, t_lo = ((m["ta_hi"], m["ta_lo"]), (m["tb_hi"], m["tb_lo"]))[part]
        count = J // n
        piece = g.piece(part, d)
        hi, lo = split(piece)
        m["w"][0:count] = hi
        m["w"][count : 2 * count] = lo
        m["w"][2 * count : 3 * count] = hi
        at = lax.rem(at + n - d, n)
        for i in range(4):
            left = jnp.concatenate([t_hi[i, at], t_hi[i, at], t_lo[i, at]], axis=1)
            product = mm(left, m["w"][0 : 3 * count]) * weight[part][i]
            if first_piece and i == 0:
                q[...] = product
            else:
                q[...] += product

    def third_place(part, own):
        q = (m["qa"], m["qb"])[part]
        cols = pl.ds(pl.multiple_of((place.core if own else 1 - place.core) * Q, Q), Q)
        for y in range(NY):
            for zp in range(NZ // 2):
                base = (y * NZ + 2 * zp) * NX * 4
                for xp in range(NX // 2):
                    even = q[base + xp * 8 : base + xp * 8 + 8, cols]
                    odd = q[base + NX * 4 + xp * 8 : base + NX * 4 + xp * 8 + 8, cols]
                    lower = jnp.where(low, even, pltpu.roll(odd, 4, 0))
                    upper = jnp.where(low, pltpu.roll(even, 4, 0), odd)
                    for k, block in enumerate((lower, upper)):
                        x = 2 * xp + k
                        if part == 0:
                            v.m["pa"][own, x, y * half + zp * 8 : y * half + zp * 8 + 8] = block
                        else:
                            v.m["pb"][own, y, x * half + zp * 8 : x * half + zp * 8 + 8] = block
        if not own:
            n, at, name = ((NX, place.x, "a"), (NY, place.y, "b"))[part]
            for d in range(1, n + 1):
                v.core_send(name, lax.rem(at + d, n))

    third_piece(0, 0, True)
    third_piece(1, 0, True)
    order = {2: (1,), 4: (1, 3, 2)}
    g.forward(0, 1)
    g.forward(1, 1)
    later = order[NX][1:]
    done = [1]
    for d in later:
        g.forward(0, d)
        g.forward(1, d)
        if d != later[-1]:
            third_piece(0, done[-1], False)
            third_piece(1, done[-1], False)
            done.append(d)
    last = [d for d in order[NX] if d not in done[:-1]]
    for part in range(2):
        for d in last:
            third_piece(part, d, False)
        third_place(part, 0)
    third_place(0, 1)
    third_place(1, 1)
    v.stage1()
    g.drain()
    g.assemble(m["s3"], m["st"])
    gram_of(m["st"], m["s3"], J, m["gram_b"], m["cross"])
    inverse = set_gram(m["gram_a"][...] * m["gram_b"][...], m["gx"])
    v.stage2()
    v.stage3()

    block = (place.y * NZ + place.z // 2 * 2) * (NX // 2) + place.x // 2
    even = m["third"][pl.ds(pl.multiple_of(block * 8, 8), 8), :]
    odd = m["third"][pl.ds(pl.multiple_of((block + NX // 2) * 8, 8), 8), :]
    low = lax.broadcasted_iota(jnp.int32, (8, R), 0) < 4
    lower = jnp.where(low, even, pltpu.roll(odd, 4, 0))
    upper = jnp.where(low, pltpu.roll(even, 4, 0), odd)
    own = jnp.where(lax.rem(place.x, 2) == 0, lower, upper)
    ahead = product_of(own, m["gx"])
    new_third = update(own, ahead, v.finish(), m["gx"], inverse)
    at = lax.rem(place.z, 2) * 4 + place.core * 2
    index = lax.broadcasted_iota(jnp.int32, (8, R), 0)
    out[8:10, :] = jnp.concatenate(
        [jnp.sum(jnp.where(index == at + k, new_third, 0.0), axis=0, keepdims=True) for k in range(2)], axis=0
    )


def hand_out(rows, out_first, out_second, out_third):
    out_first[...] = rows[0:4, :]
    out_second[...] = rows[4:8, :]
    out_third[...] = rows[8:10, :]


def sweep(devices, tensor, first, second, third):
    own, J, K = tensor.shape
    R = third.shape[1]
    shape = Shape(devices, K, R)
    NX, NY, NZ = shape.NX, shape.NY, shape.NZ
    scratch = shape.scratch()
    vmem = pl.BlockSpec(memory_space=pltpu.VMEM)
    hbm = pl.BlockSpec(memory_space=pl.ANY)
    out = pl.pallas_call(
        functools.partial(kernel, shape, tuple(scratch)),
        out_shape=jax.ShapeDtypeStruct((10, R), F32),
        in_specs=[hbm, vmem, hbm, hbm],
        out_specs=vmem,
        scratch_shapes=list(scratch.values()),
        compiler_params=pltpu.CompilerParams(collective_id=0, has_side_effects=True, vmem_limit_bytes=62 * 2**20),
    )(tensor.reshape(own, NY, NZ, NX, 8, K), first, second.reshape(NY, NZ, NX, 8, R), third)
    return pl.pallas_call(
        hand_out,
        out_shape=(
            jax.ShapeDtypeStruct((4, R), F32),
            jax.ShapeDtypeStruct((4, R), F32),
            jax.ShapeDtypeStruct((2, R), F32),
        ),
        in_specs=[vmem],
        out_specs=(vmem, vmem, vmem),
    )(out)


def solution(mesh):
    in_specs = (P("slab", None, None), P("slab", None), P(), P())
    out_specs = (P("slab", None), P("slab", None), P("slab", None))
    body = functools.partial(sweep, mesh.shape["slab"])
    return jax.shard_map(body, mesh=mesh, in_specs=in_specs, out_specs=out_specs, check_vma=False)
```

```python
import functools

import jax
import jax.numpy as jnp
from jax import lax
from jax.experimental import pallas as pl
from jax.experimental.pallas import tpu as pltpu
from jax.sharding import PartitionSpec as P

F32 = jnp.float32
BF16 = jnp.bfloat16
MESH = pl.DeviceIdType.MESH
GRIDS = {256: (4, 4, 8), 16: (2, 2, 2)}


def far_first(n):
    return sorted(range(1, n), key=lambda d: -min(d, n - d))


def mm(a, b):
    return lax.dot_general(a, b, (((1,), (0,)), ((), ())), preferred_element_type=F32)


def split(v):
    hi = v.astype(BF16)
    return hi, (v - hi.astype(F32)).astype(BF16)


def sum8(v):
    rows, cols = v.shape
    return jnp.sum(v.reshape(rows // 8, 8, cols), axis=0)


class Shape:
    def __init__(self, devices, K, R):
        self.NX, self.NY, self.NZ = GRIDS[devices]
        self.J = 8 * self.NX * self.NY * self.NZ
        self.K, self.R = K, R
        self.Q = R // 4

    def reduce_scratch(self, tag, blocks):
        NX, NY, NZ, Q = self.NX, self.NY, self.NZ, self.Q
        ra, rb, zb = NY * blocks * 8, NX * blocks * 8, blocks * 8
        dma = pltpu.SemaphoreType.DMA
        out = {
            "pa": pltpu.VMEM((2, NX, ra, Q), F32),
            "pb": pltpu.VMEM((2, NY, rb, Q), F32),
            "ca": pltpu.VMEM((NX, ra, Q), F32),
            "cb": pltpu.VMEM((NY, rb, Q), F32),
            "sa": pltpu.VMEM((NX, ra, Q), F32),
            "sb": pltpu.VMEM((NY, rb, Q), F32),
            "r1a": pltpu.VMEM((NX - 1, ra, Q), F32),
            "r1b": pltpu.VMEM((NY - 1, rb, Q), F32),
            "s2a": pltpu.VMEM((NY, zb, Q), F32),
            "s2b": pltpu.VMEM((NX, zb, Q), F32),
            "r2a": pltpu.VMEM((NY - 1, zb, Q), F32),
            "r2b": pltpu.VMEM((NX - 1, zb, Q), F32),
            "zs": pltpu.VMEM((blocks, 16, Q), F32),
            "rz": pltpu.VMEM((2, NZ, 16, Q), F32),
            "mh": pltpu.VMEM((2, 16, Q), F32),
        }
        for name, count in (("c", NX + NY), ("1a", NX - 1), ("1b", NY - 1), ("la", NX - 1), ("lb", NY - 1), ("2a", NY - 1), ("2b", NX - 1), ("z", 2 * NZ)):
            out["send_" + name] = dma((count,))
            out["recv_" + name] = dma((count,))
        return {tag + k: v for k, v in out.items()}

    def gather_scratch(self, tag):
        NX, NY, NZ, Q = self.NX, self.NY, self.NZ, self.Q
        dma = pltpu.SemaphoreType.DMA
        out = {
            "zg": pltpu.VMEM((NZ, 16, Q), F32),
            "ga": pltpu.VMEM((2, NX, NY, NZ * 8, Q), F32),
            "gb": pltpu.VMEM((2, NY, NX, NZ * 8, Q), F32),
        }
        for name, count in (("z", NZ - 1), ("2a", NY - 1), ("2b", NX - 1), ("3a", NX - 1), ("3b", NY - 1), ("4a", NX - 1), ("4b", NY - 1), ("c", NX + NY)):
            out["send_" + name] = dma((count,))
            out["recv_" + name] = dma((count,))
        return {tag + k: v for k, v in out.items()}

    def scratch(self):
        J, K, R, NX, NY, NZ, Q = self.J, self.K, self.R, self.NX, self.NY, self.NZ, self.Q
        dma = pltpu.SemaphoreType.DMA
        out = {
            "t": pltpu.VMEM((4, NX, NY, NZ, 8, K), F32),
            "second": pltpu.VMEM((NX, NY, NZ, 8, R), F32),
            "third": pltpu.VMEM((K, R), F32),
            "p": pltpu.VMEM((4, J, R), F32),
            "b3": pltpu.VMEM((3 * K, R), BF16),
            "ta_hi": pltpu.VMEM((4, NX, K, J // NX), BF16),
            "ta_lo": pltpu.VMEM((4, NX, K, J // NX), BF16),
            "tb_hi": pltpu.VMEM((4, NY, K, J // NY), BF16),
            "tb_lo": pltpu.VMEM((4, NY, K, J // NY), BF16),
            "w": pltpu.VMEM((3 * J // min(NX, NY), 2 * Q), BF16),
            "s3": pltpu.VMEM((3 * J, R), BF16),
            "st": pltpu.VMEM((R, J), BF16),
            "gram_c": pltpu.VMEM((R, R), F32),
            "gram_a": pltpu.VMEM((R, R), F32),
            "gram_b": pltpu.VMEM((R, R), F32),
            "cross": pltpu.VMEM((R, R), F32),
            "qa": pltpu.VMEM((K, 2 * Q), F32),
            "qb": pltpu.VMEM((K, 2 * Q), F32),
            "gx": pltpu.VMEM((R, 2 * R), BF16),
            "fs": pltpu.VMEM((4, 8, R), F32),
            "load_t": dma((4 * NX,)),
            "load_s": dma((NX,)),
            "load_b": dma((1,)),
        }
        out.update(self.reduce_scratch("u_", NZ))
        out.update(self.reduce_scratch("v_", NZ // 2))
        out.update(self.gather_scratch("f_"))
        out.update(self.gather_scratch("g_"))
        return out


class Place:
    def __init__(self, shape):
        self.shape = shape
        me = lax.axis_index("slab")
        self.core = lax.rem(me, 2)
        self.x = lax.rem(me // 2, shape.NX)
        self.z = lax.rem(me // (2 * shape.NX), shape.NZ)
        self.y = me // (2 * shape.NX * shape.NZ)

    def device(self, dx=0, dy=0, dz=0, dc=0):
        s = self.shape
        x, y, z = lax.rem(self.x + dx, s.NX), lax.rem(self.y + dy, s.NY), lax.rem(self.z + dz, s.NZ)
        core = lax.rem(self.core + dc, 2)
        return ((y * s.NZ + z) * s.NX + x) * 2 + core

    def partners(self):
        s = self.shape
        return (
            [self.device(dx=d) for d in range(1, s.NX)]
            + [self.device(dy=d) for d in range(1, s.NY)]
            + [self.device(dz=d) for d in range(1, s.NZ)]
            + [self.device(dc=1)]
        )


def remote(src, dst, send, recv, device):
    return pltpu.make_async_remote_copy(src, dst, send, recv, device_id=(device,), device_id_type=MESH)


class Reduce:
    def __init__(self, m, tag, place, blocks):
        self.m = {k[len(tag):]: v for k, v in m.items() if k.startswith(tag)}
        self.place, self.blocks, self.sends = place, blocks, []

    def start(self, src, dst, sem, k, device):
        copy = remote(src, dst, self.m["send_" + sem].at[k], self.m["recv_" + sem].at[k], device)
        copy.start()
        self.sends.append(copy)

    def wait(self, dst, sem, k):
        remote(dst, dst, self.m["send_" + sem].at[k], self.m["recv_" + sem].at[k], self.place.device()).wait_recv()

    def core_send(self, part, a):
        m, place = self.m, self.place
        k = a if part == "a" else place.shape.NX + a
        self.start(m["p" + part].at[0, a], m["c" + part].at[a], "c", k, place.device(dc=1))

    def stage1(self):
        m, place, s = self.m, self.place, self.place.shape
        zb = self.blocks * 8
        late = []
        for d in far_first(max(s.NX, s.NY)) + [max(s.NX, s.NY)]:
            for part, n, at, n2, at2 in (("a", s.NX, place.x, s.NY, place.y), ("b", s.NY, place.y, s.NX, place.x)):
                if d > n:
                    continue
                a = lax.rem(at + d, n)
                self.wait(m["c" + part].at[a], "c", a if part == "a" else s.NX + a)
                for e in range(n2):
                    rows = pl.ds(pl.multiple_of(lax.rem(at2 + e, n2) * zb, 8), zb)
                    m["s" + part][a, e * zb : (e + 1) * zb] = m["p" + part][1, a, rows] + m["c" + part][a, rows]
                if d < n:
                    to = place.device(dx=d) if part == "a" else place.device(dy=d)
                    rest = pl.ds(zb, (n2 - 1) * zb)
                    self.start(m["s" + part].at[a, rest], m["r1" + part].at[d - 1, rest], "1" + part, d - 1, to)
                    late.append((part, a, d, to))
        for part, a, d, to in late:
            own = pl.ds(0, zb)
            self.start(m["s" + part].at[a, own], m["r1" + part].at[d - 1, own], "l" + part, d - 1, to)

    def stage2(self):
        m, place, s = self.m, self.place, self.place.shape
        zb = self.blocks * 8
        parts = (("a", s.NX, place.x, s.NY), ("b", s.NY, place.y, s.NX))

        def total(part, n1, at1, e):
            rows = slice(e * zb, (e + 1) * zb)
            value = m["s" + part][at1, rows]
            for d in range(n1 - 1):
                value = value + m["r1" + part][d, rows]
            m["s2" + part][e] = value

        for part, n1, at1, n2 in parts:
            for d in range(n1 - 1):
                self.wait(m["r1" + part].at[d, pl.ds(zb, (n2 - 1) * zb)], "1" + part, d)
            for e in far_first(n2):
                total(part, n1, at1, e)
                to = place.device(dy=e) if part == "a" else place.device(dx=e)
                self.start(m["s2" + part].at[e], m["r2" + part].at[e - 1], "2" + part, e - 1, to)

    def stage2_own(self):
        m, place, s = self.m, self.place, self.place.shape
        zb = self.blocks * 8
        for part, n1, at1 in (("a", s.NX, place.x), ("b", s.NY, place.y)):
            for d in range(n1 - 1):
                self.wait(m["r1" + part].at[d, pl.ds(0, zb)], "l" + part, d)
            value = m["s" + part][at1, 0:zb]
            for d in range(n1 - 1):
                value = value + m["r1" + part][d, 0:zb]
            m["s2" + part][0] = value

    def stage3(self):
        m, place, s = self.m, self.place, self.place.shape
        self.stage2_own()
        for half, (part, n2) in enumerate((("a", s.NY), ("b", s.NX))):
            for e in range(n2 - 1):
                self.wait(m["r2" + part].at[e], "2" + part, e)
            total = m["s2" + part][0]
            for e in range(n2 - 1):
                total = total + m["r2" + part][e]
            m["zs"][:, half * 8 : half * 8 + 8] = total.reshape(self.blocks, 8, s.Q)
        per = s.NZ // self.blocks
        for d in far_first(s.NZ):
            block = lax.rem(place.z + d, s.NZ) // per
            self.start(m["zs"].at[block], m["rz"].at[place.core, d], "z", d, place.device(dz=d))
            self.start(m["zs"].at[block], m["rz"].at[place.core, d], "z", s.NZ + d, place.device(dz=d, dc=1))
        self.start(m["zs"].at[place.z // per], m["rz"].at[place.core, 0], "z", s.NZ, place.device(dc=1))

    def finish(self):
        m, place, s = self.m, self.place, self.place.shape
        per = s.NZ // self.blocks
        own, other = m["zs"][place.z // per], None
        for d in range(s.NZ):
            if d > 0:
                self.wait(m["rz"].at[place.core, d], "z", d)
                own = own + m["rz"][place.core, d]
            self.wait(m["rz"].at[1 - place.core, d], "z", s.NZ + d)
            piece = m["rz"][1 - place.core, d]
            other = piece if other is None else other + piece
        m["mh"][place.core] = own
        m["mh"][1 - place.core] = other
        out = jnp.concatenate([m["mh"][h, q * 8 : q * 8 + 8] for h in range(2) for q in range(2)], axis=1)
        for copy in self.sends:
            copy.wait_send()
        return out


class Gather:
    def __init__(self, m, tag, place):
        self.m = {k[len(tag):]: v for k, v in m.items() if k.startswith(tag)}
        self.place, self.sends = place, []

    start = Reduce.start
    wait = Reduce.wait

    def stage1(self, block):
        m, place, s = self.m, self.place, self.place.shape
        m["zg"][place.z] = block
        for d in far_first(s.NZ):
            self.start(m["zg"].at[place.z], m["zg"].at[place.z], "z", d - 1, place.device(dz=d))

    def stage2(self):
        m, place, s = self.m, self.place, self.place.shape
        for d in range(1, s.NZ):
            self.wait(m["zg"].at[lax.rem(place.z + s.NZ - d, s.NZ)], "z", d - 1)
        m["ga"][place.core, place.x, 0] = m["zg"][:, 0:8].reshape(s.NZ * 8, s.Q)
        m["gb"][place.core, place.y, 0] = m["zg"][:, 8:16].reshape(s.NZ * 8, s.Q)
        own_a, own_b = m["ga"].at[place.core, place.x, 0], m["gb"].at[place.core, place.y, 0]
        for e in far_first(max(s.NX, s.NY)):
            if e < s.NY:
                self.start(own_a, m["ga"].at[place.core, place.x, s.NY - e], "2a", e - 1, place.device(dy=e))
            if e < s.NX:
                self.start(own_b, m["gb"].at[place.core, place.y, s.NX - e], "2b", e - 1, place.device(dx=e))
        for e in range(1, max(s.NX, s.NY)):
            if e < s.NX:
                self.start(own_a, own_a, "3a", e - 1, place.device(dx=e))
            if e < s.NY:
                self.start(own_b, own_b, "3b", e - 1, place.device(dy=e))

    def stage3(self):
        m, place, s = self.m, self.place, self.place.shape
        for e in range(1, s.NY):
            self.wait(m["ga"].at[place.core, place.x, s.NY - e], "2a", e - 1)
        for e in range(1, s.NX):
            self.wait(m["gb"].at[place.core, place.y, s.NX - e], "2b", e - 1)
        ref, other = m["ga"].at[place.core, place.x], m["gb"].at[place.core, place.y]
        self.start(ref, ref, "c", 0, place.device(dc=1))
        self.start(other, other, "c", s.NX, place.device(dc=1))
        rest_a = m["ga"].at[place.core, place.x, pl.ds(1, s.NY - 1)]
        rest_b = m["gb"].at[place.core, place.y, pl.ds(1, s.NX - 1)]
        for d in {2: (1,), 4: (1, 3, 2)}[max(s.NX, s.NY)]:
            if d < s.NX:
                self.start(rest_a, rest_a, "4a", d - 1, place.device(dx=d))
            if d < s.NY:
                self.start(rest_b, rest_b, "4b", d - 1, place.device(dy=d))

    def forward(self, part, d):
        m, place, s = self.m, self.place, self.place.shape
        if part == 0:
            ref = m["ga"].at[place.core, lax.rem(place.x + s.NX - d, s.NX)]
            self.wait(ref.at[0], "3a", d - 1)
            self.wait(ref.at[pl.ds(1, s.NY - 1)], "4a", d - 1)
            self.start(ref, ref, "c", d, place.device(dc=1))
        else:
            ref = m["gb"].at[place.core, lax.rem(place.y + s.NY - d, s.NY)]
            self.wait(ref.at[0], "3b", d - 1)
            self.wait(ref.at[pl.ds(1, s.NX - 1)], "4b", d - 1)
            self.start(ref, ref, "c", s.NX + d, place.device(dc=1))

    def arrive(self, part, d):
        m, place, s = self.m, self.place, self.place.shape
        if part == 0:
            self.wait(m["ga"].at[1 - place.core, lax.rem(place.x + s.NX - d, s.NX)], "c", d)
        else:
            self.wait(m["gb"].at[1 - place.core, lax.rem(place.y + s.NY - d, s.NY)], "c", s.NX + d)

    def piece(self, part, d):
        m, place, s = self.m, self.place, self.place.shape
        self.arrive(part, d)
        at = lax.rem(place.x + s.NX - d, s.NX) if part == 0 else lax.rem(place.y + s.NY - d, s.NY)
        return jnp.concatenate([self.rows_a(h, at) if part == 0 else self.rows_b(h, at) for h in range(2)], axis=1)

    def rows_a(self, h, x):
        place, s = self.place, self.place.shape
        return jnp.concatenate([self.m["ga"][h, x, lax.rem(y + s.NY - place.y, s.NY)] for y in range(s.NY)], axis=0)

    def rows_b(self, h, y):
        place, s = self.place, self.place.shape
        return jnp.concatenate([self.m["gb"][h, y, lax.rem(x + s.NX - place.x, s.NX)] for x in range(s.NX)], axis=0)

    def rows_b_of(self, h, x):
        place, s = self.place, self.place.shape
        e = lax.rem(x + s.NX - place.x, s.NX)
        return jnp.concatenate([self.m["gb"][h, y, e] for y in range(s.NY)], axis=0)

    def drain(self):
        for copy in self.sends:
            copy.wait_send()

    def finish(self):
        s = self.place.shape
        for d in range(1, max(s.NX, s.NY)):
            for part, n in ((0, s.NX), (1, s.NY)):
                if d < n:
                    self.forward(part, d)
        for part, n in ((0, s.NX), (1, s.NY)):
            for d in range(n):
                self.arrive(part, d)
        self.drain()

    def assemble(self, s3, st):
        m, s = self.m, self.place.shape
        J, Q, rows = s.J, s.Q, s.NZ * 8
        per = s.NY * rows

        def step(x, carry):
            for h in range(2):
                for part in range(2):
                    cols = slice((h * 2 + part) * Q, (h * 2 + part + 1) * Q)
                    if part == 0:
                        v = self.rows_a(h, x)
                    else:
                        v = self.rows_b_of(h, x)
                    hi, lo = split(v)
                    at = pl.multiple_of(x * per, per)
                    s3[pl.ds(at, per), cols] = hi
                    s3[pl.ds(J + at, per), cols] = lo
                    s3[pl.ds(2 * J + at, per), cols] = hi
                    st[cols, pl.ds(at, per)] = v.T.astype(BF16)
            return carry

        for x in range(s.NX):
            step(x, 0)

    def assemble_first(self, s3, st):
        m, s = self.m, self.place.shape
        J, Q, per = s.J, s.Q, s.NY * s.NZ * 8
        count = per // 2
        top = lax.broadcasted_iota(jnp.int32, (per // 16, 8, Q), 1) < 4
        for h in range(2):
            for x in range(s.NX):
                at = (h * s.NX + x) * count
                for part in range(2):
                    if part == 0:
                        v = self.rows_a(h, x)
                    else:
                        v = self.rows_b_of(h, x)
                    v = v.reshape(per // 16, 2, 8, Q)
                    even, odd = v[:, 0], v[:, 1]
                    lower = jnp.where(top, even, pltpu.roll(odd, 4, 1)).reshape(count, Q)
                    upper = jnp.where(top, pltpu.roll(even, 4, 1), odd).reshape(count, Q)
                    for k, v in enumerate((lower, upper)):
                        cols = slice((part * 2 + k) * Q, (part * 2 + k + 1) * Q)
                        hi, lo = split(v)
                        s3[at : at + count, cols] = hi
                        s3[J + at : J + at + count, cols] = lo
                        st[cols, at : at + count] = v.T.astype(BF16)


def gram_of(st, s3, rows, out, cross):
    hi, lo = s3[0:rows, :], s3[rows : 2 * rows, :]
    t = st[:, 0:rows]
    cross[...] = mm(t, lo)
    out[...] = mm(t, hi)
    out[...] = out[...] + cross[...] + cross[...].T


def load_factor(get, rows, block, s3, st):
    for at in range(0, rows, block):
        v = get(at)
        hi, lo = split(v)
        s3[at : at + block, :] = hi
        s3[rows + at : rows + at + block, :] = lo
        s3[2 * rows + at : 2 * rows + at + block, :] = hi
        st[:, at : at + block] = v.T.astype(BF16)


def set_gram(g, gx):
    hi, lo = split(g)
    R = g.shape[0]
    gx[:, 0:R] = hi
    gx[:, R : 2 * R] = lo
    return 1.0 / jnp.max(jnp.sum(g, axis=0, keepdims=True), axis=1, keepdims=True)


def product_of(rows, gx):
    n, R = rows.shape
    hi = rows.astype(BF16).astype(F32)
    both = jnp.concatenate([hi, rows - hi], axis=0).astype(BF16)
    product = mm(both, gx[...])
    product = product[:n] + product[n:]
    return product[:, :R] + product[:, R:]


def update(rows, product, sums, gx, inverse):
    previous = extrapolated = updated = rows
    for turn in range(4):
        if turn > 0:
            product = product_of(extrapolated, gx)
        updated = jnp.maximum(extrapolated - (product - sums) * inverse, 0.0)
        if turn < 3:
            extrapolated = updated + turn / (turn + 3.0) * (updated - previous)
            previous = updated
    return updated


def kernel(shape, names, tensor, first, second, third, out, *refs):
    m = dict(zip(names, refs))
    s, place = shape, Place(shape)
    J, K, R, NX, NY, NZ, Q = s.J, s.K, s.R, s.NX, s.NY, s.NZ, s.Q
    per = NY * NZ * 8

    load_b = pltpu.make_async_copy(third, m["third"], m["load_b"].at[0])
    load_b.start()

    def load_t(i, x):
        return pltpu.make_async_copy(tensor.at[i, :, :, x], m["t"].at[i, x], m["load_t"].at[i * NX + x])

    def load_s(x):
        return pltpu.make_async_copy(second.at[:, :, x], m["second"].at[x], m["load_s"].at[x])

    for x in range(NX):
        load_t(0, x).start()

    barrier = pltpu.get_barrier_semaphore()
    partners = place.partners()
    for device in partners:
        pl.semaphore_signal(barrier, inc=1, device_id=(device,), device_id_type=MESH)

    load_b.wait()
    for x in range(NX):
        load_s(x).start()
    for x in range(NX):
        load_t(1, x).start()
    load_factor(lambda at: m["third"][at : at + K // 4, :], K, K // 4, m["b3"], m["st"])
    gram_of(m["st"], m["b3"], K, m["gram_c"], m["cross"])
    for i in range(4):
        for x in range(NX):
            load_t(i, x).wait()
        if i < 2:
            for x in range(NX):
                load_t(i + 2, x).start()
        hi, lo = split(m["t"][i].reshape(J, K))
        p = mm(jnp.concatenate([hi, hi, lo], axis=1), m["b3"][...])
        m["p"][i] = p
        if i == 0:
            for x in range(NX):
                load_s(x).wait()
        m["fs"][i] = sum8(p * m["second"][...].reshape(J, R))

    load_factor(lambda at: m["second"][at // per].reshape(per, R), J, per, m["s3"], m["st"])
    gram_of(m["st"], m["s3"], J, m["gram_b"], m["cross"])
    inverse = set_gram(m["gram_b"][...] * m["gram_c"][...], m["gx"])
    sums = jnp.concatenate([jnp.sum(m["fs"][i], axis=0, keepdims=True) for i in range(4)] * 2, axis=0)
    start = first[...]
    start = jnp.concatenate([start, start], axis=0)
    rows = update(start, product_of(start, m["gx"]), sums, m["gx"], inverse)
    new_first = rows[0:4]
    out[0:4, :] = new_first

    pl.semaphore_wait(barrier, len(partners))
    u = Reduce(m, "u_", place, NZ)
    v = Reduce(m, "v_", place, NZ // 2)
    f = Gather(m, "f_", place)
    g = Gather(m, "g_", place)

    top = lax.broadcasted_iota(jnp.int32, (8, Q), 0) < 4
    quarters = [rows[:, q * Q : (q + 1) * Q] for q in range(4)]
    f.stage1(jnp.concatenate([jnp.where(top, quarters[q], quarters[q + 1]) for q in (0, 2)], axis=0))

    halves = (rows[:, : 2 * Q], rows[:, 2 * Q :])
    weights = (jnp.where(place.core == 0, halves[1], halves[0]), jnp.where(place.core == 0, halves[0], halves[1]))

    def weighted(at, count, own, part):
        half = place.core if own else 1 - place.core
        cols = pl.ds(pl.multiple_of((2 * half + part) * Q, Q), Q)
        w = weights[own][:, part * Q : (part + 1) * Q]
        total = m["p"][0, pl.ds(pl.multiple_of(at, 8), count), cols] * w[0:1]
        for i in range(1, 4):
            total = total + m["p"][i, pl.ds(pl.multiple_of(at, 8), count), cols] * w[i : i + 1]
        return total

    for own in (0, 1):
        for d in far_first(max(NX, NY)) + [max(NX, NY)]:
            if d <= NX:
                a = lax.rem(place.x + d, NX)
                u.m["pa"][own, a] = weighted(a * per, per, own, 0)
                if not own:
                    u.core_send("a", a)
            if d <= NY:
                a = lax.rem(place.y + d, NY)
                for x in range(NX):
                    u.m["pb"][own, a, x * NZ * 8 : (x + 1) * NZ * 8] = weighted(x * per + a * NZ * 8, NZ * 8, own, 1)
                if not own:
                    u.core_send("b", a)
    u.stage1()

    def transpose_a(step, carry):
        i, x = step // NX, lax.rem(step, NX)
        hi, lo = split(m["t"][i, x].reshape(per, K).T)
        m["ta_hi"][i, x] = hi
        m["ta_lo"][i, x] = lo
        return carry

    def transpose_b(step, carry):
        i, y = step // NY, lax.rem(step, NY)
        hi, lo = split(m["t"][i, :, y].reshape(NX * NZ * 8, K).T)
        m["tb_hi"][i, y] = hi
        m["tb_lo"][i, y] = lo
        return carry

    f.stage2()
    lax.fori_loop(0, 4 * NX, transpose_a, 0)
    u.stage2()
    f.stage3()
    lax.fori_loop(0, 4 * NY, transpose_b, 0)
    u.stage3()
    f.finish()
    f.assemble_first(m["s3"], m["st"])
    gram_of(m["st"], m["s3"], J, m["gram_a"], m["cross"])
    inverse = set_gram(m["gram_a"][...] * m["gram_c"][...], m["gx"])
    own = m["second"][place.x, place.y, place.z]
    ahead = product_of(own, m["gx"])
    new_second = update(own, ahead, u.finish(), m["gx"], inverse)
    out[4:8, :] = jnp.where(place.core == 0, new_second[0:4], new_second[4:8])

    own = jnp.where(place.core == 0, new_second[:, : 2 * Q], new_second[:, 2 * Q :])
    g.stage1(jnp.concatenate([own[:, :Q], own[:, Q:]], axis=0))
    g.stage2()
    g.stage3()
    half = NZ // 2 * 8
    low = lax.broadcasted_iota(jnp.int32, (8, Q), 0) < 4
    weight = [
        [jnp.concatenate([rows[i : i + 1, c * Q : (c + 1) * Q] for c in (part, 2 + part)], axis=1) for i in range(4)]
        for part in range(2)
    ]

    def third_piece(part, d, first_piece):
        n, at, q = ((NX, place.x, m["qa"]), (NY, place.y, m["qb"]))[part]
        t_hi, t_lo = ((m["ta_hi"], m["ta_lo"]), (m["tb_hi"], m["tb_lo"]))[part]
        count = J // n
        piece = g.piece(part, d)
        hi, lo = split(piece)
        m["w"][0:count] = hi
        m["w"][count : 2 * count] = lo
        m["w"][2 * count : 3 * count] = hi
        at = lax.rem(at + n - d, n)
        for i in range(4):
            left = jnp.concatenate([t_hi[i, at], t_hi[i, at], t_lo[i, at]], axis=1)
            product = mm(left, m["w"][0 : 3 * count]) * weight[part][i]
            if first_piece and i == 0:
                q[...] = product
            else:
                q[...] += product

    def third_place(part, own):
        q = (m["qa"], m["qb"])[part]
        cols = pl.ds(pl.multiple_of((place.core if own else 1 - place.core) * Q, Q), Q)
        for y in range(NY):
            for zp in range(NZ // 2):
                base = (y * NZ + 2 * zp) * NX * 4
                for xp in range(NX // 2):
                    even = q[base + xp * 8 : base + xp * 8 + 8, cols]
                    odd = q[base + NX * 4 + xp * 8 : base + NX * 4 + xp * 8 + 8, cols]
                    lower = jnp.where(low, even, pltpu.roll(odd, 4, 0))
                    upper = jnp.where(low, pltpu.roll(even, 4, 0), odd)
                    for k, block in enumerate((lower, upper)):
                        x = 2 * xp + k
                        if part == 0:
                            v.m["pa"][own, x, y * half + zp * 8 : y * half + zp * 8 + 8] = block
                        else:
                            v.m["pb"][own, y, x * half + zp * 8 : x * half + zp * 8 + 8] = block
        if not own:
            n, at, name = ((NX, place.x, "a"), (NY, place.y, "b"))[part]
            for d in far_first(n) + [n]:
                v.core_send(name, lax.rem(at + d, n))

    third_piece(0, 0, True)
    third_piece(1, 0, True)
    order = {2: (1,), 4: (1, 3, 2)}
    g.forward(0, 1)
    g.forward(1, 1)
    later = order[NX][1:]
    done = [1]
    for d in later:
        g.forward(0, d)
        g.forward(1, d)
        if d != later[-1]:
            third_piece(0, done[-1], False)
            third_piece(1, done[-1], False)
            done.append(d)
    last = [d for d in order[NX] if d not in done[:-1]]
    for part in range(2):
        for d in last:
            third_piece(part, d, False)
        third_place(part, 0)
    third_place(0, 1)
    third_place(1, 1)
    v.stage1()
    g.drain()
    g.assemble(m["s3"], m["st"])
    gram_of(m["st"], m["s3"], J, m["gram_b"], m["cross"])
    inverse = set_gram(m["gram_a"][...] * m["gram_b"][...], m["gx"])
    v.stage2()
    v.stage3()

    block = (place.y * NZ + place.z // 2 * 2) * (NX // 2) + place.x // 2
    even = m["third"][pl.ds(pl.multiple_of(block * 8, 8), 8), :]
    odd = m["third"][pl.ds(pl.multiple_of((block + NX // 2) * 8, 8), 8), :]
    low = lax.broadcasted_iota(jnp.int32, (8, R), 0) < 4
    lower = jnp.where(low, even, pltpu.roll(odd, 4, 0))
    upper = jnp.where(low, pltpu.roll(even, 4, 0), odd)
    own = jnp.where(lax.rem(place.x, 2) == 0, lower, upper)
    ahead = product_of(own, m["gx"])
    new_third = update(own, ahead, v.finish(), m["gx"], inverse)
    at = lax.rem(place.z, 2) * 4 + place.core * 2
    index = lax.broadcasted_iota(jnp.int32, (8, R), 0)
    out[8:10, :] = jnp.concatenate(
        [jnp.sum(jnp.where(index == at + k, new_third, 0.0), axis=0, keepdims=True) for k in range(2)], axis=0
    )


def hand_out(rows, out_first, out_second, out_third):
    out_first[...] = rows[0:4, :]
    out_second[...] = rows[4:8, :]
    out_third[...] = rows[8:10, :]


def sweep(devices, tensor, first, second, third):
    own, J, K = tensor.shape
    R = third.shape[1]
    shape = Shape(devices, K, R)
    NX, NY, NZ = shape.NX, shape.NY, shape.NZ
    scratch = shape.scratch()
    vmem = pl.BlockSpec(memory_space=pltpu.VMEM)
    hbm = pl.BlockSpec(memory_space=pl.ANY)
    out = pl.pallas_call(
        functools.partial(kernel, shape, tuple(scratch)),
        out_shape=jax.ShapeDtypeStruct((10, R), F32),
        in_specs=[hbm, vmem, hbm, hbm],
        out_specs=vmem,
        scratch_shapes=list(scratch.values()),
        compiler_params=pltpu.CompilerParams(collective_id=0, has_side_effects=True, vmem_limit_bytes=62 * 2**20),
    )(tensor.reshape(own, NY, NZ, NX, 8, K), first, second.reshape(NY, NZ, NX, 8, R), third)
    return pl.pallas_call(
        hand_out,
        out_shape=(
            jax.ShapeDtypeStruct((4, R), F32),
            jax.ShapeDtypeStruct((4, R), F32),
            jax.ShapeDtypeStruct((2, R), F32),
        ),
        in_specs=[vmem],
        out_specs=(vmem, vmem, vmem),
    )(out)


def solution(mesh):
    in_specs = (P("slab", None, None), P("slab", None), P(), P())
    out_specs = (P("slab", None), P("slab", None), P("slab", None))
    body = functools.partial(sweep, mesh.shape["slab"])
    return jax.shard_map(body, mesh=mesh, in_specs=in_specs, out_specs=out_specs, check_vma=False)
```
